128 devices in a mesh: ctx: 16 (over z, y_lo, core), head: 8 (over x, y_hi).
Axes of the slice: x: 4, y: 4 (y_hi: 2, y_lo: 2; y = y_hi * 2 + y_lo), z: 4, core: 2. Of those that a mesh axis runs over, the one named last changes fastest.
Arguments:
- tokens: bfloat16 [3072, 2048], P('ctx', 'head'), may hold values from -6 to 6
- norm_gain: float32 [2048], replicated, may hold values from 0.25 to 1.75
- w_query: bfloat16 [2048, 2048], P(None, 'head'), may hold values from -0.125 to 0.125
- w_key: bfloat16 [2048, 2048], P(None, 'head'), may hold values from -0.125 to 0.125
- w_value: bfloat16 [2048, 2048], P(None, 'head'), may hold values from -0.125 to 0.125
- w_out: bfloat16 [2048, 2048], P('head'), may hold values from -0.125 to 0.125
- teacher: bfloat16 [3, 3072, 2048], P(None, 'ctx', 'head'), may hold values from -6 to 6
Outputs:
- grad_input: float32 [3072, 2048], P('ctx', 'head')
- grad_gain: float32 [2048], replicated
- grad_query: float32 [2048, 2048], P('ctx', 'head')
- grad_key: float32 [2048, 2048], P('ctx', 'head')
- grad_value: float32 [2048, 2048], P('ctx', 'head')
- grad_outproj: float32 [2048, 2048], P('head', 'ctx')
The draws below stay inside these ranges and needn't reach their ends.
All inputs are finite; a program needn't handle non-finite values.
Results may differ from the reference program's by a relative error of at most 0.015.
Values may be sent and summed in bfloat16 or wider, within the bound.
No kernel may reach another device: no remote copies, remote signals or barrier semaphores. Data moves between devices by JAX's collectives and lax.ppermute only.
A program may use at most 128 MiB of HBM per device.

```python
import math
import jax
import jax.numpy as jnp
from jax import lax

D = 2048
HEADS = 16
DH = 128
RECUR = 3
TOKENS = 3072


def levels(own_key, dims, split, low, top_value):
    def one(position, parts):
        draws = jax.random.uniform(jax.random.fold_in(jax.random.fold_in(own_key, 6), position), (parts,), jnp.float32, low / len(split), top_value / len(split))
        return jnp.repeat(jnp.exp(draws), dims[position] // parts).reshape((-1,) + (1,) * (len(dims) - position - 1))

    level = one(*split[0])
    for cut in split[1:]:
        level = level * one(*cut)
    return level


def centred(stream_key, dims, spread, most, shards=(), kind=jnp.bfloat16):
    loudness = levels(stream_key, dims, shards, -0.22, 0.18) if shards else 1.0
    array = jax.random.normal(stream_key, dims, jnp.float32) * spread * loudness
    return jnp.minimum(jnp.maximum(array, -most), most).astype(kind)


def setup_inputs(seed: int = 0) -> dict:
    key_of = jax.random.split(jax.random.key(seed), 8)
    tokens = centred(key_of[0], (TOKENS, D), 1.0, 6.0, ((0, 16), (1, 8)))
    norm_gain = jnp.clip(1.0 + 0.15 * jax.random.normal(key_of[1], (D,), jnp.float32), 0.25, 1.75)
    w_query = centred(key_of[2], (D, HEADS * DH), D ** -0.5, 0.125, ((1, 8),))
    w_key = centred(key_of[3], (D, HEADS * DH), D ** -0.5, 0.125, ((1, 8),))
    w_value = centred(key_of[4], (D, HEADS * DH), D ** -0.5, 0.125, ((1, 8),))
    w_out = centred(key_of[5], (HEADS * DH, D), (HEADS * DH) ** -0.5, 0.125, ((0, 8),))
    teacher = centred(key_of[6], (RECUR, TOKENS, D), 1.0, 6.0, ((1, 16), (2, 8)))
    return {"tokens": tokens, "norm_gain": norm_gain, "w_query": w_query, "w_key": w_key, "w_value": w_value, "w_out": w_out, "teacher": teacher}


EPSILON = 1e-06
MASKED = -1e+30

def normalize(state, norm_gain):
    inverse = lax.rsqrt(lax.optimization_barrier(jnp.mean(state * state, axis=-1, keepdims=True)) + EPSILON)
    scaled = state * inverse
    return ((scaled * norm_gain).astype(jnp.bfloat16), scaled, inverse)

def split_heads(block):
    return jnp.transpose(block.reshape(block.shape[0], -1, DH), (1, 0, 2))

def join_heads(block):
    return jnp.transpose(block, (1, 0, 2)).reshape(block.shape[1], -1)

def masked_scores(query, key_block, query_pos, key_pos):
    scaling = 1.0 / math.sqrt(query.shape[-1])
    scores = jnp.dot(query, key_block.T, preferred_element_type=jnp.float32) * scaling
    return jnp.where(key_pos[None, :] <= query_pos[:, None], scores, MASKED)

def attend(query, key_block, value_block, query_pos, key_pos):
    scores = masked_scores(query, key_block, query_pos, key_pos)
    row_max = lax.optimization_barrier(jnp.max(scores, axis=-1, keepdims=True))
    weights = jnp.exp(scores - row_max)
    denominator = lax.optimization_barrier(jnp.sum(weights, axis=-1, keepdims=True))
    probabilities = (weights / denominator).astype(jnp.bfloat16)
    attended = jnp.dot(probabilities, value_block, preferred_element_type=jnp.float32).astype(jnp.bfloat16)
    return (attended, row_max[:, 0] + jnp.log(denominator[:, 0]))

def score_grads(query, key_block, value_block, grad_attended, row_dot, log_total, query_pos, key_pos):
    scores = masked_scores(query, key_block, query_pos, key_pos)
    probabilities = jnp.exp(scores - log_total[:, None])
    grad_probs = jnp.dot(grad_attended, value_block.T, preferred_element_type=jnp.float32)
    grad_scores = (probabilities * (grad_probs - row_dot[:, None])).astype(jnp.bfloat16)
    return (probabilities.astype(jnp.bfloat16), grad_scores)

def both_grads(query, key_block, value_block, grad_attended, row_dot, log_total, query_pos, key_pos):
    scaling = 1.0 / math.sqrt(query.shape[-1])
    rounded, grad_scores = score_grads(query, key_block, value_block, grad_attended, row_dot, log_total, query_pos, key_pos)
    grad_rows = (jnp.dot(grad_scores, key_block, preferred_element_type=jnp.float32) * scaling).astype(jnp.bfloat16)
    key_term = jnp.dot(grad_scores.T, query, preferred_element_type=jnp.float32) * scaling
    value_term = jnp.dot(rounded.T, grad_attended, preferred_element_type=jnp.float32)
    return (grad_rows, key_term, value_term)

def reference(tokens, norm_gain, w_query, w_key, w_value, w_out, teacher):
    positions = jnp.arange(TOKENS, dtype=jnp.int32)
    state = tokens.astype(jnp.float32)
    states = [state]
    normed_list = []
    scaled_list = []
    inverses = []
    queries = []
    attended_list = []
    totals = []
    for level in range(RECUR):
        normed, scaled, inverse = normalize(state, norm_gain)
        query_rows = jnp.dot(normed, w_query, preferred_element_type=jnp.float32).astype(jnp.bfloat16)
        if level == 0:
            key_heads = split_heads(jnp.dot(normed, w_key, preferred_element_type=jnp.float32).astype(jnp.bfloat16))
            value_heads = split_heads(jnp.dot(normed, w_value, preferred_element_type=jnp.float32).astype(jnp.bfloat16))
        attended_heads, log_total = lax.map(lambda pieces: attend(pieces[0], pieces[1], pieces[2], positions, positions), (split_heads(query_rows), key_heads, value_heads))
        attended = join_heads(attended_heads)
        state = state + jnp.dot(attended, w_out, preferred_element_type=jnp.float32)
        states.append(state)
        normed_list.append(normed)
        scaled_list.append(scaled)
        inverses.append(inverse)
        queries.append(query_rows)
        attended_list.append(attended)
        totals.append(log_total)
    weight = 1.0 / math.sqrt(TOKENS)
    width = HEADS * DH
    grad = jnp.zeros((TOKENS, D), jnp.float32)
    grad_query = jnp.zeros((D, width), jnp.float32)
    grad_outproj = jnp.zeros((width, D), jnp.float32)
    grad_gain = jnp.zeros((D,), jnp.float32)
    key_sum = jnp.zeros((HEADS, TOKENS, DH), jnp.float32)
    value_sum = jnp.zeros((HEADS, TOKENS, DH), jnp.float32)
    for level in range(RECUR - 1, -1, -1):
        grad = grad + weight * (states[level + 1] - teacher[level].astype(jnp.float32))
        grad_round = grad.astype(jnp.bfloat16)
        grad_outproj = grad_outproj + jnp.dot(attended_list[level].T, grad_round, preferred_element_type=jnp.float32)
        grad_attended = jnp.dot(grad_round, w_out.T, preferred_element_type=jnp.float32).astype(jnp.bfloat16)
        grad_heads = split_heads(grad_attended)
        row_dot = lax.optimization_barrier(jnp.sum(grad_heads.astype(jnp.float32) * split_heads(attended_list[level]).astype(jnp.float32), axis=-1))
        grad_query_heads, key_term, value_term = lax.map(lambda pieces: both_grads(pieces[0], pieces[1], pieces[2], pieces[3], pieces[4], pieces[5], positions, positions), (split_heads(queries[level]), key_heads, value_heads, grad_heads, row_dot, totals[level]))
        key_sum = key_sum + key_term
        value_sum = value_sum + value_term
        grad_query_rows = join_heads(grad_query_heads)
        grad_normed = jnp.dot(grad_query_rows, w_query.T, preferred_element_type=jnp.float32)
        grad_query = grad_query + jnp.dot(normed_list[level].T, grad_query_rows, preferred_element_type=jnp.float32)
        if level == 0:
            grad_keys = join_heads(key_sum).astype(jnp.bfloat16)
            grad_values = join_heads(value_sum).astype(jnp.bfloat16)
            grad_normed = grad_normed + jnp.dot(grad_keys, w_key.T, preferred_element_type=jnp.float32)
            grad_normed = grad_normed + jnp.dot(grad_values, w_value.T, preferred_element_type=jnp.float32)
            grad_key = jnp.dot(normed_list[0].T, grad_keys, preferred_element_type=jnp.float32)
            grad_value = jnp.dot(normed_list[0].T, grad_values, preferred_element_type=jnp.float32)
        scaled = scaled_list[level]
        grad_gain = grad_gain + lax.optimization_barrier(jnp.sum(grad_normed * scaled, axis=0))
        back = grad_normed * norm_gain
        grad = grad + inverses[level] * (back - scaled * lax.optimization_barrier(jnp.mean(back * scaled, axis=-1, keepdims=True)))
    return (grad, grad_gain, grad_query, grad_key, grad_value, grad_outproj)
```

```python
import math

import jax
import jax.numpy as jnp
from jax import lax
from jax.sharding import PartitionSpec as P

DH = 128
RECUR = 3

EPSILON = 1e-06
MASKED = -1e30
F32 = jnp.float32
BF16 = jnp.bfloat16


def dot(a, b):
    return jnp.dot(a, b, preferred_element_type=F32)


def dot_tn(a, b):
    return lax.dot_general(a, b, (((0,), (0,)), ((), ())), preferred_element_type=F32)


def dot_nt(a, b):
    return lax.dot_general(a, b, (((1,), (1,)), ((), ())), preferred_element_type=F32)


def inverse_of(state):
    return lax.rsqrt(jnp.mean(state * state, axis=-1, keepdims=True) + EPSILON)


def split_heads(block):
    return jnp.transpose(block.reshape(block.shape[0], -1, DH), (1, 0, 2))


def join_heads(block):
    return jnp.transpose(block, (1, 0, 2)).reshape(block.shape[1], -1)


def masked_scores(query, key_block, query_pos, key_pos):
    scaling = 1.0 / math.sqrt(query.shape[-1])
    scores = dot_nt(query, key_block) * scaling
    return jnp.where(key_pos[None, :] <= query_pos[:, None], scores, MASKED)


def attend(query, key_block, value_block, query_pos, key_pos):
    scores = masked_scores(query, key_block, query_pos, key_pos)
    row_max = jnp.max(scores, axis=-1, keepdims=True)
    weights = jnp.exp(scores - row_max)
    denominator = jnp.sum(weights, axis=-1, keepdims=True)
    probabilities = (weights / denominator).astype(BF16)
    attended = dot(probabilities, value_block).astype(BF16)
    return (attended, row_max[:, 0] + jnp.log(denominator[:, 0]))


def both_grads(query, key_block, value_block, grad_attended, row_dot, log_total, query_pos, key_pos):
    scaling = 1.0 / math.sqrt(query.shape[-1])
    scores = masked_scores(query, key_block, query_pos, key_pos)
    probabilities = jnp.exp(scores - log_total[:, None])
    grad_probs = dot_nt(grad_attended, value_block)
    grad_scores = (probabilities * (grad_probs - row_dot[:, None])).astype(BF16)
    grad_rows = (dot(grad_scores, key_block) * scaling).astype(BF16)
    key_term = dot_tn(grad_scores, query) * scaling
    value_term = dot_tn(probabilities.astype(BF16), grad_attended)
    return (grad_rows, key_term, value_term)


def body(tokens, norm_gain, w_query, w_key, w_value, w_out, teacher):
    rows, width = tokens.shape
    shards = lax.axis_size("ctx")
    heads = lax.axis_size("head")
    model = w_query.shape[0]
    chips = shards // 2
    ctx = lax.axis_index("ctx")
    head = lax.axis_index("head")
    core = ctx % 2
    same_core = [[2 * i + c for i in range(chips)] for c in range(2)]
    sibling = [(i, i ^ 1) for i in range(shards)]

    def gather_heads(x):
        return lax.all_to_all(jnp.broadcast_to(x[None], (heads,) + x.shape), "head", 0, 0)

    def whole_rows(x):
        got = gather_heads(x)
        return jnp.transpose(got, (1, 0, 2)).reshape(x.shape[0], -1)

    def swap(x):
        return lax.ppermute(x, "ctx", sibling)

    def gather_weight(w):
        half = w.shape[0] // 2
        mine = lax.all_gather(lax.dynamic_slice_in_dim(w, core * half, half, 0), "head", axis=0)
        mine = mine.reshape(heads * half, -1)
        return mine, swap(mine)

    def times_weight(x, weight):
        cut = x.reshape(rows, heads, 2, width // 2)
        here = lax.dynamic_index_in_dim(cut, core, 2, keepdims=False).reshape(rows, -1)
        there = lax.dynamic_index_in_dim(cut, 1 - core, 2, keepdims=False).reshape(rows, -1)
        return dot(here, weight[0]) + dot(there, weight[1])

    out_whole = gather_weight(w_out)
    teacher_whole = lax.all_gather(teacher, "head", axis=0)
    query_back = gather_weight(w_query.T)

    query_pos = ctx * rows + jnp.arange(rows, dtype=jnp.int32)
    chip_start = jnp.arange(chips, dtype=jnp.int32) * (2 * rows)
    block_start = jnp.concatenate([chip_start + core * rows, chip_start + (1 - core) * rows])
    key_pos = (block_start[:, None] + jnp.arange(rows, dtype=jnp.int32)[None, :]).reshape(-1)

    head_map = (0, 0, 0, None, None)
    grad_map = (0, 0, 0, 0, 0, 0, None, None)
    state = whole_rows(tokens).astype(F32)
    states, inverses, normed_list, queries, attended_list, totals = [state], [], [], [], [], []
    for level in range(RECUR):
        inverse = inverse_of(state)
        normed = (state * inverse * norm_gain).astype(BF16)
        query_rows = dot(normed, w_query).astype(BF16)
        if level == 0:
            own = jnp.concatenate([dot(normed, w_key).astype(BF16), dot(normed, w_value).astype(BF16)], 1)
            mine = lax.all_to_all(
                jnp.broadcast_to(own[None], (chips,) + own.shape), "ctx", 0, 0, axis_index_groups=same_core
            )
            both = jnp.concatenate([mine, swap(mine)], 0).reshape(shards * rows, 2 * width)
            key_heads = split_heads(both[:, :width])
            value_heads = split_heads(both[:, width:])
        attended_heads, log_total = jax.vmap(attend, in_axes=head_map)(
            split_heads(query_rows), key_heads, value_heads, query_pos, key_pos
        )
        attended = join_heads(attended_heads)
        state = state + times_weight(whole_rows(attended), out_whole)
        states.append(state)
        inverses.append(inverse)
        normed_list.append(normed)
        queries.append(query_rows)
        attended_list.append(attended)
        totals.append(log_total)

    weight = 1.0 / math.sqrt(rows * shards)
    own_columns = (jnp.arange(model, dtype=jnp.int32) // width == head).astype(F32)
    grad = jnp.zeros_like(state)
    gain_sum = jnp.zeros((model,), F32)
    key_sum = 0.0
    value_sum = 0.0
    grad_rounds, grad_queries = [], []
    for level in range(RECUR - 1, -1, -1):
        wanted = jnp.transpose(teacher_whole[:, level], (1, 0, 2)).reshape(rows, model)
        grad = grad + weight * (states[level + 1] - wanted.astype(F32))
        grad_round = grad.astype(BF16)
        grad_rounds.append(grad_round)
        grad_attended = dot_nt(grad_round, w_out).astype(BF16)
        grad_heads = split_heads(grad_attended)
        row_dot = jnp.sum(grad_heads.astype(F32) * split_heads(attended_list[level]).astype(F32), axis=-1)
        grad_query_heads, key_term, value_term = jax.vmap(both_grads, in_axes=grad_map)(
            split_heads(queries[level]),
            key_heads,
            value_heads,
            grad_heads,
            row_dot,
            totals[level],
            query_pos,
            key_pos,
        )
        key_sum = key_sum + key_term
        value_sum = value_sum + value_term
        grad_query_rows = join_heads(grad_query_heads)
        grad_queries.append(grad_query_rows)
        scaled = states[level] * inverses[level]
        if level > 0:
            grad_normed = times_weight(whole_rows(grad_query_rows), query_back)
        else:
            sums = jnp.concatenate([join_heads(key_sum), join_heads(value_sum)], 1).astype(BF16)
            sums = sums.reshape(2, chips, rows, 2 * width)
            pair = (sums[0].astype(F32) + swap(sums[1]).astype(F32)).astype(BF16)
            parts = lax.all_to_all(pair, "ctx", 0, 0, axis_index_groups=same_core)
            own_grads = jnp.sum(parts.astype(F32), axis=0).astype(BF16)
            grad_normed = dot_nt(grad_query_rows, w_query)
            grad_normed = grad_normed + dot_nt(own_grads[:, :width], w_key)
            grad_normed = grad_normed + dot_nt(own_grads[:, width:], w_value)
        gain_term = jnp.sum(grad_normed * scaled, axis=0)
        gain_sum = gain_sum + (gain_term * own_columns if level > 0 else gain_term)
        back = grad_normed * norm_gain
        step = inverses[level] * (back - scaled * jnp.mean(back * scaled, axis=-1, keepdims=True))
        if level > 0:
            grad = grad + step

    grad_query = dot_tn(
        jnp.concatenate([normed_list[2], normed_list[1], normed_list[0]], 0), jnp.concatenate(grad_queries, 0)
    )
    grad_out = dot_tn(
        jnp.concatenate(grad_rounds, 0),
        jnp.concatenate([attended_list[2], attended_list[1], attended_list[0]], 0),
    )
    grad_both = dot_tn(normed_list[0], own_grads)
    partial = jnp.concatenate([grad_query, grad_out, grad_both], 1).astype(BF16)
    slab = model // shards
    partial = partial.reshape(chips, 2, slab, 4 * width)
    gain_rows = gain_sum.reshape(-1, 4 * width).astype(BF16)
    gain_rows = jnp.broadcast_to(gain_rows[None], (chips,) + gain_rows.shape)
    here = lax.dynamic_index_in_dim(partial, core, 1, keepdims=False)
    there = lax.dynamic_index_in_dim(partial, 1 - core, 1, keepdims=False)
    here = jnp.concatenate([here, gain_rows], 1).astype(F32)
    there = swap(jnp.concatenate([there, gain_rows], 1)).astype(F32)
    parts = lax.all_to_all((here + there).astype(BF16), "ctx", 0, 0, axis_index_groups=same_core)
    summed = jnp.sum(parts.astype(F32), axis=0)
    gain_rows = summed[slab:].reshape(-1, width).astype(BF16)
    summed = summed[:slab]

    step = jnp.transpose(step.reshape(rows, heads, width), (1, 0, 2)).astype(BF16)
    gain_rows = jnp.broadcast_to(gain_rows[None], (heads,) + gain_rows.shape)
    parts = lax.all_to_all(jnp.concatenate([step, gain_rows], 1), "head", 0, 0)
    last = jnp.sum(parts.astype(F32), axis=0)
    grad_gain = last[rows:].reshape(-1)
    grad_input = lax.dynamic_slice_in_dim(grad, head * width, width, 1) + last[:rows]
    return (
        grad_input,
        grad_gain,
        summed[:, :width],
        summed[:, 2 * width : 3 * width],
        summed[:, 3 * width :],
        summed[:, width : 2 * width].T,
    )


def solution(mesh):
    return jax.shard_map(
        body,
        mesh=mesh,
        in_specs=(
            P("ctx", "head"),
            P(),
            P(None, "head"),
            P(None, "head"),
            P(None, "head"),
            P("head", None),
            P(None, "ctx", "head"),
        ),
        out_specs=(
            P("ctx", "head"),
            P(),
            P("ctx", "head"),
            P("ctx", "head"),
            P("ctx", "head"),
            P("head", "ctx"),
        ),
        check_vma=False,
    )
```

```python
import functools
import math

import jax
import jax.numpy as jnp
from jax import lax
from jax.experimental import pallas as pl
from jax.experimental.pallas import tpu as pltpu
from jax.sharding import PartitionSpec as P

DH = 128
RECUR = 3

EPSILON = 1e-06
MASKED = -1e30
F32 = jnp.float32
BF16 = jnp.bfloat16
SCALING = 1.0 / math.sqrt(DH)
LOG2E = math.log2(math.e)
SMEM = pl.BlockSpec(memory_space=pltpu.SMEM)
ANY = pl.BlockSpec(memory_space=pltpu.HBM)
BLOCK = 512
CHUNK = 4
INVERSE = 2


def dot(a, b):
    return jnp.dot(a, b, preferred_element_type=F32)


def dot_tn(a, b):
    return lax.dot_general(a, b, (((0,), (0,)), ((), ())), preferred_element_type=F32)


def dot_nt(a, b):
    return lax.dot_general(a, b, (((1,), (1,)), ((), ())), preferred_element_type=F32)


def shape(dims, kind):
    return jax.ShapeDtypeStruct(dims, kind)


class Fetched:
    def __init__(self, src, dst, sem):
        self.copy = pltpu.make_async_copy(src, dst, sem)
        self.dst = dst
        self.waited = False

    def start(self):
        self.copy.start()

    def ref(self):
        if not self.waited:
            self.copy.wait()
            self.waited = True
        return self.dst


class Result:
    def __init__(self, ref, out, sems):
        self.ref, self.out, self.sems, self.copies = ref, out, sems, []

    def send(self, *views):
        for src, dst in views or ((self.ref, self.out),):
            copy = pltpu.make_async_copy(src, dst, self.sems.at[len(self.copies)])
            copy.start()
            self.copies.append(copy)


def call(kernel, results, cost, place, early, late=(), raw=(), scratch=()):
    n_early, n_late, n_raw, n_out, n_scratch = len(early), len(late), len(raw), len(results), len(scratch)
    parts = [x[1:] if isinstance(x, tuple) else None for x in [*early, *late]]
    early, late = ([x[0] if isinstance(x, tuple) else x for x in group] for group in (early, late))

    def inner(*refs):
        refs = list(refs)

        def take(count):
            taken, refs[:] = refs[:count], refs[count:]
            return taken

        place_ref = take(1)[0]
        early_src, late_src, raw_ref, out = take(n_early), take(n_late), take(n_raw), take(n_out)
        early_src = [ref.at[part[0], 0 : part[1]] if part else ref for ref, part in zip(early_src, parts)]
        late_src = [ref.at[part[0], 0 : part[1]] if part else ref for ref, part in zip(late_src, parts[n_early:])]
        early_dst, late_dst, out_ref, more = take(n_early), take(n_late), take(n_out), take(n_scratch)
        in_sems, out_sems = refs[0], refs[1:]
        first = [Fetched(s, d, in_sems.at[i]) for i, (s, d) in enumerate(zip(early_src, early_dst))]
        then = [Fetched(s, d, in_sems.at[n_early + i]) for i, (s, d) in enumerate(zip(late_src, late_dst))]
        ends = [Result(r, o, s) for r, o, s in zip(out_ref, out, out_sems)]
        for item in first:
            item.start()
        kernel(place_ref, first, then, raw_ref, ends, more)
        for item in first + then:
            item.ref()
        for end in ends:
            for copy in end.copies:
                copy.wait()

    def vmem(x, part=None):
        return pltpu.VMEM((part[1], *x.shape[2:]) if part else x.shape, x.dtype)

    return pl.pallas_call(
        inner,
        out_shape=[r[1] for r in results],
        in_specs=[SMEM] + [ANY] * (n_early + n_late + n_raw),
        out_specs=[pl.BlockSpec(memory_space=pltpu.HBM)] * n_out,
        scratch_shapes=[vmem(x, part) for x, part in zip([*early, *late], parts)]
        + [vmem(r[0]) for r in results]
        + list(scratch)
        + [pltpu.SemaphoreType.DMA((max(1, n_early + n_late),))]
        + [pltpu.SemaphoreType.DMA((r[2],)) for r in results],
        compiler_params=pltpu.CompilerParams(vmem_limit_bytes=52 * 1024 * 1024),
        cost_estimate=pl.CostEstimate(flops=cost[0], bytes_accessed=cost[1], transcendentals=cost[2]),
    )(place, *early, *late, *raw)


def same(dims, kind):
    return (shape(dims, kind), shape(dims, kind), 1)


def start_all(items):
    for item in items:
        item.start()


def fetch_out_weight(place, raw, weight, sems):
    core = lax.rem(place[0], 2)
    half = raw[0].shape[1]
    blocks = []
    for start in range(0, raw[0].shape[2], BLOCK):
        columns = pl.ds(start, BLOCK)
        block = []
        group = 0
        for j, ref in enumerate(raw):
            parity = core if j == 0 else 1 - core
            rows = pl.ds(pl.multiple_of(parity * half, half), half)
            sem = sems.at[len(raw) * (start // BLOCK) + j]
            groups = pl.ds(group, ref.shape[0])
            block.append(pltpu.make_async_copy(ref.at[:, :, columns], weight.at[groups, rows, columns], sem))
            group = group + ref.shape[0] if j else 0
        start_all(block)
        blocks.append(block)
    return blocks


def fetch_query_weight(place, raw, weight, sems):
    core = lax.rem(place[0], 2)
    half = raw[0].shape[1]
    blocks = []
    for ref, parity in ((raw[0], core), (raw[1], 1 - core)):
        for start in range(0, half, BLOCK):
            rows = pl.ds(pl.multiple_of(parity * half + start, BLOCK), BLOCK)
            copy = pltpu.make_async_copy(ref.at[:, pl.ds(start, BLOCK), :], weight.at[:, rows, :], sems.at[len(blocks)])
            copy.start()
            blocks.append((copy, rows))
    return blocks


def wait_all(copies):
    for copy in copies:
        copy.wait()


def lanes_joined(ref, rows):
    return jnp.concatenate([ref[i, :rows, :] for i in range(ref.shape[0])], axis=1)


def key_position(shape_, axis, rows, chunk, half, core):
    index = lax.broadcasted_iota(jnp.int32, shape_, axis)
    gap = jnp.zeros(shape_, jnp.int32)
    for i in range(1, CHUNK):
        gap = gap + jnp.where(index >= i * rows, rows, 0)
    first = chunk * CHUNK
    start = 2 * (first % half) * rows + (core if first < half else 1 - core) * rows
    return index + gap + start


def chunk_of(kv, chunk, column):
    half = kv[0].shape[0]
    ref = kv[0] if chunk * CHUNK < half else kv[1]
    first = chunk * CHUNK % half
    return ref[first : first + CHUNK, :, column : column + DH].reshape(-1, DH)


def chunks_of(kv):
    return 2 * kv[0].shape[0] // CHUNK


def send_spread(result, cut):
    if len(result.out.shape) == 2:
        result.send((result.ref.at[:, cut], result.out.at[:, cut]))
        return
    rows = slice(0, result.ref.shape[0])
    result.send(*[(result.ref.at[:, cut], result.out.at[i, rows, cut]) for i in range(result.out.shape[0])])


def send_below(result, rider):
    rows = pl.ds(result.ref.shape[0], rider.shape[0])
    result.send(*[(rider, result.out.at[i, rows, :]) for i in range(result.out.shape[0])])


def attention(ctx, query, kv, scores, attended):
    rows, width = query.shape
    core = lax.rem(ctx, 2)
    span = CHUNK * rows
    query_pos = ctx * rows + lax.broadcasted_iota(jnp.int32, (rows, 1), 0)
    lane = lax.broadcasted_iota(jnp.int32, (rows, DH), 1)
    logs = jnp.zeros((rows, DH), F32)
    for head in range(width // DH):
        cut = slice(head * DH, (head + 1) * DH)
        rows_q = query[:, cut]
        row_max = jnp.full((rows, 1), MASKED, F32)
        for chunk in range(chunks_of(kv)):
            key_pos = key_position((1, span), 1, rows, chunk, kv[0].shape[0], core)
            part = dot_nt(rows_q, chunk_of(kv, chunk, head * DH)) * (SCALING * LOG2E)
            part = jnp.where(key_pos <= query_pos, part, MASKED)
            scores[:, chunk * span : (chunk + 1) * span] = part
            row_max = jnp.maximum(row_max, jnp.max(part, axis=1, keepdims=True))
        total = jnp.zeros((rows, 1), F32)
        out = jnp.zeros((rows, DH), F32)
        for chunk in range(chunks_of(kv)):
            part = jnp.exp2(scores[:, chunk * span : (chunk + 1) * span] - row_max)
            total = total + jnp.sum(part, axis=1, keepdims=True)
            out = out + dot(part.astype(BF16), chunk_of(kv, chunk, width + head * DH))
        attended.ref[:, cut] = (out / total).astype(BF16)
        send_spread(attended, cut)
        logs = jnp.where(lane == head, row_max + jnp.log2(total), logs)
    return logs


def attention_back(ctx, query, kv, grad_attended, attended, logs, grad_query):
    rows, width = query.shape
    core = lax.rem(ctx, 2)
    span = CHUNK * rows
    query_pos = ctx * rows + lax.broadcasted_iota(jnp.int32, (rows, 1), 0)
    for head in range(width // DH):
        cut = slice(head * DH, (head + 1) * DH)
        rows_q, rows_g = query[:, cut], grad_attended[:, cut]
        row_dot = jnp.sum(rows_g.astype(F32) * attended[:, cut].astype(F32), axis=1, keepdims=True)
        log_total = logs[:, head : head + 1]
        out = jnp.zeros((rows, DH), F32)
        for chunk in range(chunks_of(kv)):
            key_pos = key_position((1, span), 1, rows, chunk, kv[0].shape[0], core)
            keys = chunk_of(kv, chunk, head * DH)
            part = dot_nt(rows_q, keys) * (SCALING * LOG2E)
            part = jnp.exp2(jnp.where(key_pos <= query_pos, part, MASKED) - log_total)
            grad_probs = dot_nt(rows_g, chunk_of(kv, chunk, width + head * DH))
            out = out + dot((part * (grad_probs - row_dot)).astype(BF16), keys)
        grad_query.ref[:, cut] = (out * SCALING).astype(BF16)
        send_spread(grad_query, cut)


def turned(picks, columns):
    total = jnp.zeros((picks.shape[0], columns.shape[0]), F32)
    for _ in range(3):
        piece = columns.astype(BF16)
        columns = columns - piece.astype(F32)
        total = total + dot_nt(picks, piece)
    return total


def key_back(ctx, query, kv, grad_attended, attended, logs, prior, store):
    rows, width = query.shape
    core = lax.rem(ctx, 2)
    span = CHUNK * rows
    query_pos = ctx * rows + lax.broadcasted_iota(jnp.int32, (1, rows), 1)
    picks = (lax.broadcasted_iota(jnp.int32, (8, DH), 0) == lax.broadcasted_iota(jnp.int32, (8, DH), 1)).astype(BF16)
    log_rows = turned(picks, logs)
    row_dots = []
    for head in range(width // DH):
        cut = slice(head * DH, (head + 1) * DH)
        product = grad_attended[:, cut].astype(F32) * attended[:, cut].astype(F32)
        row_dots.append(turned(jnp.ones((8, DH), BF16), product)[0:1])
    for chunk in range(chunks_of(kv)):
        key_pos = key_position((span, 1), 0, rows, chunk, kv[0].shape[0], core)
        for head in range(width // DH):
            cut = slice(head * DH, (head + 1) * DH)
            rows_q, rows_g = query[:, cut], grad_attended[:, cut]
            part = dot_nt(chunk_of(kv, chunk, head * DH), rows_q) * (SCALING * LOG2E)
            part = jnp.exp2(jnp.where(key_pos <= query_pos, part, MASKED) - log_rows[head : head + 1, :])
            grad_probs = dot_nt(chunk_of(kv, chunk, width + head * DH), rows_g)
            key_term = dot((part * (grad_probs - row_dots[head])).astype(BF16), rows_q) * SCALING
            value_term = dot(part.astype(BF16), rows_g)
            for term, column in ((key_term, head * DH), (value_term, width + head * DH)):
                term = term.reshape(CHUNK, rows, DH)
                if prior is not None:
                    term = term + prior[chunk * CHUNK : (chunk + 1) * CHUNK, :, column : column + DH]
                store(chunk, column, term)


def project_state(gathered, state, weight, blocks, state_out):
    whole = lanes_joined(gathered, state.shape[0])
    squares = jnp.zeros((whole.shape[0], 1), F32)
    for start in range(0, state.shape[1], BLOCK):
        wait_all(blocks[start // BLOCK])
        columns = slice(start, start + BLOCK)
        new = state[:, columns] + dot(whole, weight[:, :, columns].reshape(whole.shape[1], BLOCK))
        state_out[:, columns] = new
        squares = squares + jnp.sum(new * new, axis=1, keepdims=True)
    return squares


def normalize_rows(squares, state, gain, normed):
    model = state.shape[1]
    inverse = lax.rsqrt(squares / model + EPSILON)
    for start in range(0, model, BLOCK):
        columns = slice(start, start + BLOCK)
        normed[:, columns] = (state[:, columns] * inverse * gain[0:1, columns]).astype(BF16)
    return inverse


def enter_kernel(place, early, late, raw, results, scratch):
    gathered, gain, w_key, w_value, w_query = early
    state, normed, stats, query, own = results
    rows = state.ref.shape[0]
    squares = jnp.zeros((rows, 1), F32)
    got = gathered.ref()
    width = got.shape[2]
    for i in range(got.shape[0]):
        part = got[i].astype(F32)
        state.ref[:, i * width : (i + 1) * width] = part
        squares = squares + jnp.sum(part * part, axis=1, keepdims=True)
    state.send()
    inverse = normalize_rows(squares, state.ref, gain.ref(), normed.ref)
    normed.send()
    stats.ref[...] = jnp.broadcast_to(inverse, stats.ref.shape)
    stats.send()
    for weight, cut in ((w_key, slice(0, width)), (w_value, slice(width, 2 * width))):
        own.ref[:, cut] = dot(normed.ref[...], weight.ref()[...]).astype(BF16)
        send_spread(own, cut)
    query.ref[...] = dot(normed.ref[...], w_query.ref()[...]).astype(BF16)
    query.send()


def first_kernel(place, early, late, raw, results, scratch):
    query = early[0].ref()[...]
    start_all(late)
    attended, stats = results
    stats.ref[...] = attention(place[0], query, (late[0].ref(), late[1].ref()), scratch[0], attended)
    stats.send()


def level_kernel(place, early, late, raw, results, scratch):
    gathered, state, gain = early
    weight, scores, sems = scratch
    state_out, normed, query, attended, stats = results
    blocks = fetch_out_weight(place, raw, weight, sems)
    start_all(late)
    w_query, kv_mine, kv_other = late[:3]
    squares = project_state(gathered.ref(), state.ref(), weight, blocks, state_out.ref)
    state_out.send()
    inverse = normalize_rows(squares, state_out.ref, gain.ref(), normed.ref)
    normed.send()
    rows = dot(normed.ref[...], w_query.ref()[...]).astype(BF16)
    query.ref[...] = rows
    query.send()
    logs = attention(place[0], rows, (kv_mine.ref(), kv_other.ref()), scores, attended)
    lane = lax.broadcasted_iota(jnp.int32, logs.shape, 1)
    stats.ref[...] = jnp.where(lane == INVERSE, inverse, logs)
    stats.send()
    if len(late) > 3:
        send_below(attended, late[3].ref())


def turn_kernel(loss_weight, place, early, late, raw, results, scratch):
    gathered, state = early
    weight, state_new, sems = scratch
    grad, grad_round, grad_attended, grad_query = results
    rows = state_new.shape[0]
    blocks = fetch_out_weight(place, raw, weight, sems)
    start_all(late)
    kv_mine, kv_other, query, attended, logs, rider = late
    got = gathered.ref()
    project_state(got, state.ref(), weight, blocks, state_new)
    width = got.shape[2]
    for i in range(got.shape[0]):
        columns = slice(i * width, (i + 1) * width)
        new = loss_weight * (state_new[:, columns] - got[i, rows:, :].astype(F32))
        grad.ref[:, columns] = new
        grad_round.ref[:, columns] = new.astype(BF16)
    grad.send()
    grad_round.send()
    send_below(grad_query, rider.ref())
    out = dot_nt(grad_round.ref[...], weight[place[1]]).astype(BF16)
    grad_attended.ref[...] = out
    grad_attended.send()
    attention_back(
        place[0], query.ref()[...], (kv_mine.ref(), kv_other.ref()), out, attended.ref()[...], logs.ref()[...], grad_query
    )


def norm_back(gathered, state, inv, gain, grad, loss_weight, weight, blocks, scratch, grad_out, round_out, gain_out):
    rows, model = state.shape
    count = gathered.shape[0]
    mean = jnp.zeros((rows, 1), F32)
    for copy, columns in blocks:
        copy.wait()
        normed = dot_nt(gathered[0, :rows, :], weight[0, columns, :])
        for h in range(1, count):
            normed = normed + dot_nt(gathered[h, :rows, :], weight[h, columns, :])
        term = normed * (state[:, columns] * inv)
        gain_out[:, columns] = jnp.broadcast_to(jnp.sum(term, axis=0, keepdims=True), (8, BLOCK))
        mean = mean + jnp.sum(term * gain[0:1, columns], axis=1, keepdims=True)
        scratch[:, columns] = normed
    mean = mean / model
    width = gathered.shape[2]
    for i in range(count):
        columns = slice(i * width, (i + 1) * width)
        here = state[:, columns]
        new = grad[:, columns] + inv * (scratch[:, columns] * gain[0:1, columns] - here * inv * mean)
        new = new + loss_weight * (here - gathered[i, rows:, :].astype(F32))
        grad_out[:, columns] = new
        round_out[:, columns] = new.astype(BF16)


def back_kernel(level, loss_weight, place, early, late, raw, results, scratch):
    gathered, state, stats, gain, grad = early
    weight, back, sems = scratch
    blocks = fetch_query_weight(place, raw, weight, sems)
    start_all(late)
    w_out, kv_mine, kv_other, query, attended, extra = late[:6]
    grad_out, grad_round, grad_attended, gain_out = results[:4]
    inv = stats.ref()[:, INVERSE : INVERSE + 1]
    norm_back(
        gathered.ref(), state.ref(), inv, gain.ref(), grad.ref(), loss_weight, weight, blocks, back,
        grad_out.ref, grad_round.ref, gain_out.ref,
    )
    grad_out.send()
    grad_round.send()
    gain_out.send()
    out = dot_nt(grad_round.ref[...], w_out.ref()[...]).astype(BF16)
    grad_attended.ref[...] = out
    grad_attended.send()
    kv = (kv_mine.ref(), kv_other.ref())
    if level > 0:
        send_below(results[4], late[6].ref())
        attention_back(place[0], query.ref()[...], kv, out, attended.ref()[...], extra.ref()[...], results[4])
        return
    half = kv[0].shape[0]

    def store(chunk, column, term):
        end = results[4] if chunk * CHUNK < half else results[5]
        first = chunk * CHUNK % half
        end.ref[first : first + CHUNK, :, column : column + DH] = term.astype(BF16)
        if chunk * CHUNK == half and column == 0:
            results[4].send()

    key_back(place[0], query.ref()[...], kv, out, attended.ref()[...], extra.ref()[...], late[6].ref(), store)
    results[5].send()


def keys_kernel(place, early, late, raw, results, scratch):
    query, grad_attended, attended, logs = [item.ref()[...] for item in early]
    start_all(late)
    kv = (late[0].ref(), late[1].ref())
    prior = late[2].ref() if len(late) > 2 else None
    sums = results[0]

    def store(chunk, column, term):
        sums.ref[chunk * CHUNK : (chunk + 1) * CHUNK, :, column : column + DH] = term

    key_back(place[0], query, kv, grad_attended, attended, logs, prior, store)
    sums.send()


def query_kernel(place, early, late, raw, results, scratch):
    query, grad_attended, attended, logs = [item.ref()[...] for item in early]
    start_all(late)
    kv_mine, kv_other = late[0].ref(), late[1].ref()
    grad_query, here, there = results
    attention_back(place[0], query, (kv_mine, kv_other), grad_attended, attended, logs, grad_query)
    refs = [item.ref() for item in late[2:]]
    count = (len(refs) - 2) // 4 + 1
    normeds, rounds, attendeds, queries = (
        refs[:count],
        refs[count : 2 * count],
        [attended] + refs[2 * count : 3 * count - 1],
        [grad_query.ref[...]] + refs[3 * count - 1 :],
    )
    width = query.shape[1]
    core = lax.rem(place[0], 2)
    slab = here.ref.shape[1]
    for end, parity in ((there, 1 - core), (here, core)):
        for i in range(end.ref.shape[0]):
            block = pl.ds(pl.multiple_of((2 * i + parity) * slab, slab), slab)
            for lhs, rhs, start in ((normeds, queries, 0), (rounds, attendeds, width)):
                total = dot_tn(lhs[0][:, block], rhs[0][...])
                for a, b in zip(lhs[1:], rhs[1:]):
                    total = total + dot_tn(a[:, block], b[...])
                end.ref[i, :, start : start + width] = total.astype(BF16)
        end.send()


def leave_kernel(place, early, late, raw, results, scratch):
    parts, grad_query, state, stats, gain, w_query, w_key, w_value, normed, *gain_terms = early
    there, here = results[:2]
    steps = results[2:]
    back = scratch[0]
    rows, model = back.shape
    width = grad_query.dst.shape[1]
    got = parts.ref()
    own = got[0].astype(F32)
    for i in range(1, got.shape[0]):
        own = own + got[i].astype(F32)
    own = own.astype(BF16)
    inv = stats.ref()[:, INVERSE : INVERSE + 1]
    head = place[1]
    mean = jnp.zeros((rows, 1), F32)
    gain_rows = []
    for start in range(0, model, BLOCK):
        columns = slice(start, start + BLOCK)
        part = dot_nt(grad_query.ref()[...], w_query.ref()[columns, :])
        part = part + dot_nt(own[:, :width], w_key.ref()[columns, :])
        part = part + dot_nt(own[:, width:], w_value.ref()[columns, :])
        term = part * (state.ref()[:, columns] * inv)
        feature = start + lax.broadcasted_iota(jnp.int32, (1, BLOCK), 1)
        mine = jnp.logical_and(feature >= head * width, feature < (head + 1) * width)
        before = gain_terms[0].ref()[0:1, columns]
        for term_before in gain_terms[1:]:
            before = before + term_before.ref()[0:1, columns]
        before = jnp.where(mine, before, 0.0)
        gain_rows.append(jnp.sum(term, axis=0, keepdims=True) + before)
        mean = mean + jnp.sum(term * gain.ref()[0:1, columns], axis=1, keepdims=True)
        back[:, columns] = part
    mean = mean / model
    count = here.ref.shape[0]
    slab = model // (2 * count)
    pad = here.ref.shape[1] - slab
    row = lax.broadcasted_iota(jnp.int32, (pad, BLOCK), 0)
    tail = jnp.zeros((pad, BLOCK), F32)
    for i, value in enumerate(gain_rows):
        tail = jnp.where(row == i, jnp.broadcast_to(value, tail.shape), tail)
    tail = tail.astype(BF16)
    core = lax.rem(place[0], 2)
    for end, parity in ((there, 1 - core), (here, core)):
        for i in range(count):
            block = pl.ds(pl.multiple_of((2 * i + parity) * slab, slab), slab)
            end.ref[i, :slab, :] = dot_tn(normed.ref()[:, block], own).astype(BF16)
            end.ref[i, slab:, :] = tail
        end.send()
    for k, step in enumerate(steps):
        columns = pl.ds(pl.multiple_of(lax.bitwise_xor(head, k) * width, width), width)
        factor = gain.ref()[0:1, columns]
        new = inv * (back[:, columns] * factor - state.ref()[:, columns] * inv * mean)
        step.ref[...] = new.astype(BF16)
        step.send()


def pair_kernel(place, early, late, raw, results, scratch):
    refs = [item.ref() for item in early]
    out = results[0]
    for i in range(out.ref.shape[0]):
        start = 0
        for here, there in zip(refs[::2], refs[1::2]):
            total = here[i].astype(F32) + there[i].astype(F32)
            out.ref[i, start : start + total.shape[0], :] = total.astype(BF16)
            start += total.shape[0]
    out.send()


def middle_kernel(place, early, late, raw, results, scratch):
    grad, sem = scratch
    rows, width = grad.shape
    columns = pl.ds(pl.multiple_of(place[1] * width, width), width)
    copy = pltpu.make_async_copy(raw[0].at[:, columns], grad, sem.at[0])
    copy.start()
    got = early[0].ref()
    gain, grad_input, grad_query, grad_out, grad_key, grad_value = results
    slab = grad_query.ref.shape[0]
    total = got[0].astype(F32)
    for i in range(1, got.shape[0]):
        total = total + got[i].astype(F32)
    row = lax.broadcasted_iota(jnp.int32, gain.ref.shape, 0)
    tail = jnp.zeros(gain.ref.shape, F32)
    for i in range(gain.out.shape[0]):
        value = total[2 * slab + i // 2 : 2 * slab + i // 2 + 1, (i % 2) * width : (i % 2 + 1) * width]
        tail = jnp.where(row == i, jnp.broadcast_to(value, tail.shape), tail)
    gain.ref[...] = tail.astype(BF16)
    gain.send(*[(gain.ref, gain.out.at[i]) for i in range(gain.out.shape[0])])
    grad_query.ref[...] = total[:slab, :width]
    grad_out.ref[...] = jnp.transpose(total[:slab, width:])
    grad_key.ref[...] = total[slab : 2 * slab, :width]
    grad_value.ref[...] = total[slab : 2 * slab, width:]
    for end in results[2:]:
        end.send()
    step = early[1].ref()[...].astype(F32)
    for item in early[2:]:
        step = step + item.ref()[...].astype(F32)
    copy.wait()
    grad_input.ref[...] = grad[...] + step
    grad_input.send()


def last_kernel(place, early, late, raw, results, scratch):
    got = early[0].ref()
    total = got[0].astype(F32)
    for i in range(1, got.shape[0]):
        total = total + got[i].astype(F32)
    results[0].ref[...] = total[: results[0].ref.shape[0]]
    results[0].send()


def body(tokens, norm_gain, w_query, w_key, w_value, w_out, teacher):
    rows, width = tokens.shape
    shards = lax.axis_size("ctx")
    heads = lax.axis_size("head")
    model = w_query.shape[0]
    chips = shards // 2
    slab = model // shards
    ctx = lax.axis_index("ctx")
    head = lax.axis_index("head")
    core = ctx % 2
    same_core = [[2 * i + c for i in range(chips)] for c in range(2)]
    sibling = [(i, i ^ 1) for i in range(shards)]
    loss_weight = 1.0 / math.sqrt(rows * shards)
    dma = pltpu.SemaphoreType.DMA

    def spread(x, count):
        return jnp.broadcast_to(x[None], (count,) + x.shape)

    def over_heads(x):
        return lax.all_to_all(x, "head", 0, 0)

    def over_chips(x):
        return lax.all_to_all(x, "ctx", 0, 0, axis_index_groups=same_core)

    def swap(x):
        return lax.ppermute(x, "ctx", sibling)

    def after(x, *others):
        return lax.optimization_barrier((x,) + others)[0]

    place = jnp.stack([ctx, head]).astype(jnp.int32)
    gain = jnp.broadcast_to(norm_gain.reshape(1, model), (8, model))

    out_mine = lax.all_gather(lax.dynamic_slice_in_dim(w_out, core * (width // 2), width // 2, 0), "head", axis=0)
    back_mine = lax.all_gather(lax.dynamic_slice_in_dim(w_query, core * (model // 2), model // 2, 0), "head", axis=0)
    first = over_heads(spread(tokens, heads))

    wide = same((rows, model), F32)
    thin = same((rows, model), BF16)
    own_shape = same((rows, width), BF16)
    sent = (shape((rows, width), BF16), shape((heads, rows, width), BF16), heads * (width // DH))
    taller = (shape((rows, width), BF16), shape((heads, 2 * rows, width), BF16), heads * (width // DH + 1))
    stats_shape = same((rows, DH), F32)
    score_scratch = pltpu.VMEM((rows, rows * shards), F32)
    weight_scratch = pltpu.VMEM((heads, width, model), BF16)
    back_scratch = pltpu.VMEM((heads, model, width), BF16)
    out_sems = 2 * (model // BLOCK)
    wide_scratch = pltpu.VMEM((rows, model), F32)
    pairs = rows * rows * shards * (width // DH)
    matmul = 2 * pairs * DH
    projection = 2 * rows * model * model
    small = projection // heads

    state, normed, stats, query, own = call(
        enter_kernel,
        [
            wide,
            thin,
            stats_shape,
            own_shape,
            (shape((rows, 2 * width), BF16), shape((chips, rows, 2 * width), BF16), 2 * chips),
        ],
        (3 * small, 8 << 20, 0),
        place, [first, gain, w_key, w_value, w_query],
    )
    kv_mine = over_chips(own)
    kv = [kv_mine, swap(kv_mine)]
    sent_rows, logs = call(
        first_kernel,
        [sent, stats_shape],
        (2 * matmul, 5 << 20, pairs),
        place, [query], kv, scratch=[score_scratch],
    )
    states, normeds, queries, attendeds = [state], [normed], [query], [sent_rows]
    stats_list, logs_list = [stats], [logs]
    out_mine = after(out_mine, sent_rows)
    out_raw = [out_mine, swap(out_mine)]
    for level in range(1, RECUR):
        last_one = level == RECUR - 1
        state, normed, query, sent_rows, stats = call(
            level_kernel,
            [wide, thin, own_shape, taller if last_one else sent, stats_shape],
            (projection + small + 2 * matmul, 18 << 20, pairs),
            place, [over_heads(sent_rows), states[-1], gain],
            [w_query, *kv] + ([(teacher, level, rows)] if last_one else []), out_raw,
            [weight_scratch, score_scratch, dma((out_sems,))],
        )
        states.append(state)
        normeds.append(normed)
        queries.append(query)
        attendeds.append(sent_rows)
        stats_list.append(stats)
        logs_list.append(stats)
    own_attended = [(rows_, 0, rows) for rows_ in attendeds]

    gathered = over_heads(sent_rows)
    back_mine = after(back_mine, gathered)
    back_raw = [back_mine, swap(back_mine)]
    level = RECUR - 1
    grad, grad_round, grad_attended, sent_rows = call(
        functools.partial(turn_kernel, loss_weight),
        [wide, thin, own_shape, taller],
        (projection + small + 3 * matmul, 18 << 20, pairs),
        place, [gathered, states[level]],
        [*kv, queries[level], own_attended[level], logs_list[level], (teacher, level - 1, rows)],
        out_raw,
        [weight_scratch, wide_scratch, dma((out_sems,))],
    )
    grad_rounds, grad_queries, grad_attendeds = [grad_round], [(sent_rows, 0, rows)], [grad_attended]
    gain_terms = []
    sums = []
    for level in range(RECUR - 2, -1, -1):
        gathered = over_heads(after(sent_rows, *sums) if sums else sent_rows)
        up = level + 1
        sums = call(
            keys_kernel,
            [same((shards, rows, 2 * width), F32)],
            (4 * matmul, 16 << 20, pairs),
            place, [queries[up], grad_attendeds[-1], own_attended[up], logs_list[up]], [*kv, *sums],
        )
        results = [wide, thin, own_shape, same((8, model), F32)]
        late = [w_out, *kv, queries[level], own_attended[level], logs_list[level]]
        if level > 0:
            results = results + [taller]
            late = late + [(teacher, level - 1, rows)]
        else:
            results = results + [same((chips, rows, 2 * width), BF16)] * 2
            late = late + list(sums)
        grad, grad_round, grad_attended, gain_term, sent_rows, *sent_other = call(
            functools.partial(back_kernel, level, loss_weight),
            results,
            (projection + small + 4 * matmul, 20 << 20, pairs),
            place, [gathered, states[up], stats_list[up], gain, grad], late, back_raw,
            [back_scratch, wide_scratch, dma((model // BLOCK,))],
        )
        gain_terms.append(gain_term)
        grad_rounds.append(grad_round)
        grad_attendeds.append(grad_attended)
        if level > 0:
            grad_queries.append((sent_rows, 0, rows))

    def add_pairs(*arrays):
        tall = sum(x.shape[1] for x in arrays[::2])
        total = same((chips, tall, 2 * width), BF16)
        return call(pair_kernel, [total], (1 << 20, 6 << 20, 0), place, arrays)[0]

    pair = (sent_rows.astype(F32) + swap(sent_other[0]).astype(F32)).astype(BF16)
    parts = over_chips(pair)
    query_first = after(queries[0], pair)
    last_query, here, there = call(
        query_kernel,
        [(own_shape[0], own_shape[1], width // DH)] + [same((chips, slab, 2 * width), BF16)] * 2,
        (5 * matmul, 16 << 20, pairs),
        place, [query_first, grad_attendeds[-1], own_attended[0], logs_list[0]],
        [*kv, *normeds, *grad_rounds[::-1], *own_attended[1:], *grad_queries[::-1]],
    )
    early = (here, swap(there))

    pad = 16
    there, here, *steps = call(
        leave_kernel,
        [same((chips, slab + pad, 2 * width), BF16)] * 2 + [own_shape] * heads,
        (6 * small, 12 << 20, 0),
        place,
        [parts, last_query, states[0], stats_list[0], gain, w_query, w_key, w_value, normeds[0], *gain_terms],
        scratch=[wide_scratch],
    )
    both = add_pairs(*early, here, swap(there))
    steps = [
        lax.ppermute(step, "head", [(i, i ^ k) for i in range(heads)]) if k else step for k, step in enumerate(steps)
    ]
    gain_rows, grad_input, grad_query, grad_out, grad_key, grad_value = call(
        middle_kernel,
        [
            (shape((pad, width), BF16), shape((heads, pad, width), BF16), heads),
            same((rows, width), F32),
            same((slab, width), F32),
            same((width, slab), F32),
            same((slab, width), F32),
            same((slab, width), F32),
        ],
        (1 << 20, 6 << 20, 0),
        place, [over_chips(both), *steps], raw=[grad], scratch=[pltpu.VMEM((rows, width), F32), dma((1,))],
    )
    grad_gain = call(
        last_kernel,
        [same((model // width, width), F32)],
        (1 << 16, 1 << 17, 0),
        place, [over_heads(gain_rows)],
    )[0]
    return (grad_input, grad_gain.reshape(-1), grad_query, grad_key, grad_value, grad_out)


def solution(mesh):
    return jax.shard_map(
        body,
        mesh=mesh,
        in_specs=(
            P("ctx", "head"),
            P(),
            P(None, "head"),
            P(None, "head"),
            P(None, "head"),
            P("head", None),
            P(None, "ctx", "head"),
        ),
        out_specs=(
            P("ctx", "head"),
            P(),
            P("ctx", "head"),
            P("ctx", "head"),
            P("ctx", "head"),
            P("head", "ctx"),
        ),
        check_vma=False,
    )
```

```python
import functools
import math

import jax
import jax.numpy as jnp
from jax import lax
from jax.experimental import pallas as pl
from jax.experimental.pallas import tpu as pltpu
from jax.sharding import PartitionSpec as P

DH = 128
RECUR = 3

EPSILON = 1e-06
MASKED = -1e30
F32 = jnp.float32
BF16 = jnp.bfloat16
SCALING = 1.0 / math.sqrt(DH)
LOG2E = math.log2(math.e)
SMEM = pl.BlockSpec(memory_space=pltpu.SMEM)
ANY = pl.BlockSpec(memory_space=pl.ANY)
BLOCK = 512
CHUNK = 4
INVERSE = 2


def dot(a, b):
    return jnp.dot(a, b, preferred_element_type=F32)


def dot_tn(a, b):
    return lax.dot_general(a, b, (((0,), (0,)), ((), ())), preferred_element_type=F32)


def dot_nt(a, b):
    return lax.dot_general(a, b, (((1,), (1,)), ((), ())), preferred_element_type=F32)


def shape(dims, kind):
    return jax.ShapeDtypeStruct(dims, kind)


class Fetched:
    def __init__(self, src, dst, sem):
        self.copy = pltpu.make_async_copy(src, dst, sem)
        self.dst = dst
        self.waited = False

    def start(self):
        self.copy.start()

    def ref(self):
        if not self.waited:
            self.copy.wait()
            self.waited = True
        return self.dst


class Result:
    def __init__(self, ref, out, sems):
        self.ref, self.out, self.sems, self.copies = ref, out, sems, []

    def send(self, *views):
        for src, dst in views or ((self.ref, self.out),):
            copy = pltpu.make_async_copy(src, dst, self.sems.at[len(self.copies)])
            copy.start()
            self.copies.append(copy)


def call(kernel, results, cost, place, early, late=(), raw=(), scratch=()):
    n_early, n_late, n_raw, n_out, n_scratch = len(early), len(late), len(raw), len(results), len(scratch)
    parts = [x[1:] if isinstance(x, tuple) else None for x in [*early, *late]]
    early, late = ([x[0] if isinstance(x, tuple) else x for x in group] for group in (early, late))

    def inner(*refs):
        refs = list(refs)

        def take(count):
            taken, refs[:] = refs[:count], refs[count:]
            return taken

        place_ref = take(1)[0]
        early_src, late_src, raw_ref, out = take(n_early), take(n_late), take(n_raw), take(n_out)
        early_src = [ref.at[part[0], 0 : part[1]] if part else ref for ref, part in zip(early_src, parts)]
        late_src = [ref.at[part[0], 0 : part[1]] if part else ref for ref, part in zip(late_src, parts[n_early:])]
        early_dst, late_dst, out_ref, more = take(n_early), take(n_late), take(n_out), take(n_scratch)
        in_sems, out_sems = refs[0], refs[1:]
        first = [Fetched(s, d, in_sems.at[i]) for i, (s, d) in enumerate(zip(early_src, early_dst))]
        then = [Fetched(s, d, in_sems.at[n_early + i]) for i, (s, d) in enumerate(zip(late_src, late_dst))]
        ends = [Result(r, o, s) for r, o, s in zip(out_ref, out, out_sems)]
        for item in first:
            item.start()
        kernel(place_ref, first, then, raw_ref, ends, more)
        for item in first + then:
            item.ref()
        for end in ends:
            for copy in end.copies:
                copy.wait()

    def vmem(x, part=None):
        return pltpu.VMEM((part[1], *x.shape[2:]) if part else x.shape, x.dtype)

    return pl.pallas_call(
        inner,
        out_shape=[r[1] for r in results],
        in_specs=[SMEM] + [ANY] * (n_early + n_late + n_raw),
        out_specs=[pl.BlockSpec(memory_space=pltpu.HBM)] * n_out,
        scratch_shapes=[vmem(x, part) for x, part in zip([*early, *late], parts)]
        + [vmem(r[0]) for r in results]
        + list(scratch)
        + [pltpu.SemaphoreType.DMA((max(1, n_early + n_late),))]
        + [pltpu.SemaphoreType.DMA((r[2],)) for r in results],
        compiler_params=pltpu.CompilerParams(vmem_limit_bytes=52 * 1024 * 1024),
        cost_estimate=pl.CostEstimate(flops=cost[0], bytes_accessed=cost[1], transcendentals=cost[2]),
    )(place, *early, *late, *raw)


def same(dims, kind):
    return (shape(dims, kind), shape(dims, kind), 1)


def start_all(items):
    for item in items:
        item.start()


def fetch_out_weight(place, raw, weight, sems):
    core = lax.rem(place[0], 2)
    half = raw[0].shape[1]
    blocks = []
    for start in range(0, raw[0].shape[2], BLOCK):
        columns = pl.ds(start, BLOCK)
        block = []
        group = 0
        for j, ref in enumerate(raw):
            parity = core if j == 0 else 1 - core
            rows = pl.ds(pl.multiple_of(parity * half, half), half)
            sem = sems.at[len(raw) * (start // BLOCK) + j]
            groups = pl.ds(group, ref.shape[0])
            block.append(pltpu.make_async_copy(ref.at[:, :, columns], weight.at[groups, rows, columns], sem))
            group = group + ref.shape[0] if j else 0
        start_all(block)
        blocks.append(block)
    return blocks


def fetch_query_weight(place, raw, weight, sems):
    core = lax.rem(place[0], 2)
    half = raw[0].shape[1]
    blocks = []
    for ref, parity in ((raw[0], core), (raw[1], 1 - core)):
        for start in range(0, half, BLOCK):
            rows = pl.ds(pl.multiple_of(parity * half + start, BLOCK), BLOCK)
            copy = pltpu.make_async_copy(ref.at[:, pl.ds(start, BLOCK), :], weight.at[:, rows, :], sems.at[len(blocks)])
            copy.start()
            blocks.append((copy, rows))
    return blocks


def wait_all(copies):
    for copy in copies:
        copy.wait()


def lanes_joined(ref, rows):
    return jnp.concatenate([ref[i, :rows, :] for i in range(ref.shape[0])], axis=1)


def key_position(shape_, axis, rows, chunk, half, core):
    index = lax.broadcasted_iota(jnp.int32, shape_, axis)
    gap = jnp.zeros(shape_, jnp.int32)
    for i in range(1, CHUNK):
        gap = gap + jnp.where(index >= i * rows, rows, 0)
    first = chunk * CHUNK
    start = 2 * (first % half) * rows + (core if first < half else 1 - core) * rows
    return index + gap + start


def chunk_of(kv, chunk, column):
    half = kv[0].shape[0]
    ref = kv[0] if chunk * CHUNK < half else kv[1]
    first = chunk * CHUNK % half
    return ref[first : first + CHUNK, :, column : column + DH].reshape(-1, DH)


def chunks_of(kv):
    return 2 * kv[0].shape[0] // CHUNK


def send_spread(result, cut):
    if len(result.out.shape) == 2:
        result.send((result.ref.at[:, cut], result.out.at[:, cut]))
        return
    rows = slice(0, result.ref.shape[0])
    result.send(*[(result.ref.at[:, cut], result.out.at[i, rows, cut]) for i in range(result.out.shape[0])])


def send_below(result, rider):
    rows = pl.ds(result.ref.shape[0], rider.shape[0])
    result.send(*[(rider, result.out.at[i, rows, :]) for i in range(result.out.shape[0])])


def attention(ctx, query, kv, scores, attended):
    rows, width = query.shape
    core = lax.rem(ctx, 2)
    span = CHUNK * rows
    query_pos = ctx * rows + lax.broadcasted_iota(jnp.int32, (rows, 1), 0)
    lane = lax.broadcasted_iota(jnp.int32, (rows, DH), 1)
    logs = jnp.zeros((rows, DH), F32)
    for head in range(width // DH):
        cut = slice(head * DH, (head + 1) * DH)
        rows_q = query[:, cut]
        row_max = jnp.full((rows, 1), MASKED, F32)
        for chunk in range(chunks_of(kv)):
            key_pos = key_position((1, span), 1, rows, chunk, kv[0].shape[0], core)
            part = dot_nt(rows_q, chunk_of(kv, chunk, head * DH)) * (SCALING * LOG2E)
            part = jnp.where(key_pos <= query_pos, part, MASKED)
            scores[:, chunk * span : (chunk + 1) * span] = part
            row_max = jnp.maximum(row_max, jnp.max(part, axis=1, keepdims=True))
        total = jnp.zeros((rows, 1), F32)
        out = jnp.zeros((rows, DH), F32)
        for chunk in range(chunks_of(kv)):
            part = jnp.exp2(scores[:, chunk * span : (chunk + 1) * span] - row_max)
            total = total + jnp.sum(part, axis=1, keepdims=True)
            out = out + dot(part.astype(BF16), chunk_of(kv, chunk, width + head * DH))
        attended.ref[:, cut] = (out / total).astype(BF16)
        send_spread(attended, cut)
        logs = jnp.where(lane == head, row_max + jnp.log2(total), logs)
    return logs


def attention_back(ctx, query, kv, grad_attended, attended, logs, grad_query):
    rows, width = query.shape
    core = lax.rem(ctx, 2)
    span = CHUNK * rows
    query_pos = ctx * rows + lax.broadcasted_iota(jnp.int32, (rows, 1), 0)
    for head in range(width // DH):
        cut = slice(head * DH, (head + 1) * DH)
        rows_q, rows_g = query[:, cut], grad_attended[:, cut]
        row_dot = jnp.sum(rows_g.astype(F32) * attended[:, cut].astype(F32), axis=1, keepdims=True)
        log_total = logs[:, head : head + 1]
        out = jnp.zeros((rows, DH), F32)
        for chunk in range(chunks_of(kv)):
            key_pos = key_position((1, span), 1, rows, chunk, kv[0].shape[0], core)
            keys = chunk_of(kv, chunk, head * DH)
            part = dot_nt(rows_q, keys) * (SCALING * LOG2E)
            part = jnp.exp2(jnp.where(key_pos <= query_pos, part, MASKED) - log_total)
            grad_probs = dot_nt(rows_g, chunk_of(kv, chunk, width + head * DH))
            out = out + dot((part * (grad_probs - row_dot)).astype(BF16), keys)
        grad_query.ref[:, cut] = (out * SCALING).astype(BF16)
        send_spread(grad_query, cut)


def turned(picks, columns):
    total = jnp.zeros((picks.shape[0], columns.shape[0]), F32)
    for _ in range(3):
        piece = columns.astype(BF16)
        columns = columns - piece.astype(F32)
        total = total + dot_nt(picks, piece)
    return total


def key_back(ctx, query, kv, grad_attended, attended, logs, prior, store):
    rows, width = query.shape
    core = lax.rem(ctx, 2)
    span = CHUNK * rows
    query_pos = ctx * rows + lax.broadcasted_iota(jnp.int32, (1, rows), 1)
    picks = (lax.broadcasted_iota(jnp.int32, (8, DH), 0) == lax.broadcasted_iota(jnp.int32, (8, DH), 1)).astype(BF16)
    log_rows = turned(picks, logs)
    row_dots = []
    for head in range(width // DH):
        cut = slice(head * DH, (head + 1) * DH)
        product = grad_attended[:, cut].astype(F32) * attended[:, cut].astype(F32)
        row_dots.append(turned(jnp.ones((8, DH), BF16), product)[0:1])
    for chunk in range(chunks_of(kv)):
        key_pos = key_position((span, 1), 0, rows, chunk, kv[0].shape[0], core)
        for head in range(width // DH):
            cut = slice(head * DH, (head + 1) * DH)
            rows_q, rows_g = query[:, cut], grad_attended[:, cut]
            part = dot_nt(chunk_of(kv, chunk, head * DH), rows_q) * (SCALING * LOG2E)
            part = jnp.exp2(jnp.where(key_pos <= query_pos, part, MASKED) - log_rows[head : head + 1, :])
            grad_probs = dot_nt(chunk_of(kv, chunk, width + head * DH), rows_g)
            key_term = dot((part * (grad_probs - row_dots[head])).astype(BF16), rows_q) * SCALING
            value_term = dot(part.astype(BF16), rows_g)
            for term, column in ((key_term, head * DH), (value_term, width + head * DH)):
                term = term.reshape(CHUNK, rows, DH)
                if prior is not None:
                    term = term + prior[chunk * CHUNK : (chunk + 1) * CHUNK, :, column : column + DH]
                store(chunk, column, term)


def project_state(gathered, state, weight, blocks, state_out):
    whole = lanes_joined(gathered, state.shape[0])
    squares = jnp.zeros((whole.shape[0], 1), F32)
    for start in range(0, state.shape[1], BLOCK):
        wait_all(blocks[start // BLOCK])
        columns = slice(start, start + BLOCK)
        new = state[:, columns] + dot(whole, weight[:, :, columns].reshape(whole.shape[1], BLOCK))
        state_out[:, columns] = new
        squares = squares + jnp.sum(new * new, axis=1, keepdims=True)
    return squares


def normalize_rows(squares, state, gain, normed):
    model = state.shape[1]
    inverse = lax.rsqrt(squares / model + EPSILON)
    for start in range(0, model, BLOCK):
        columns = slice(start, start + BLOCK)
        normed[:, columns] = (state[:, columns] * inverse * gain[0:1, columns]).astype(BF16)
    return inverse


def enter_kernel(place, early, late, raw, results, scratch):
    gathered, gain, w_key, w_value, w_query = early
    state, normed, stats, query, own = results
    rows = state.ref.shape[0]
    squares = jnp.zeros((rows, 1), F32)
    got = gathered.ref()
    width = got.shape[2]
    for i in range(got.shape[0]):
        part = got[i].astype(F32)
        state.ref[:, i * width : (i + 1) * width] = part
        squares = squares + jnp.sum(part * part, axis=1, keepdims=True)
    state.send()
    inverse = normalize_rows(squares, state.ref, gain.ref(), normed.ref)
    normed.send()
    stats.ref[...] = jnp.broadcast_to(inverse, stats.ref.shape)
    stats.send()
    for weight, cut in ((w_key, slice(0, width)), (w_value, slice(width, 2 * width))):
        own.ref[:, cut] = dot(normed.ref[...], weight.ref()[...]).astype(BF16)
        send_spread(own, cut)
    query.ref[...] = dot(normed.ref[...], w_query.ref()[...]).astype(BF16)
    query.send()


def first_kernel(place, early, late, raw, results, scratch):
    query = early[0].ref()[...]
    start_all(late)
    attended, stats = results
    send_below(attended, late[2].ref())
    stats.ref[...] = attention(place[0], query, (late[0].ref(), late[1].ref()), scratch[0], attended)
    stats.send()


def level_kernel(place, early, late, raw, results, scratch):
    gathered, state, gain = early
    weight, scores, sems = scratch
    state_out, normed, query, attended, stats = results
    blocks = fetch_out_weight(place, raw, weight, sems)
    start_all(late)
    w_query, kv_mine, kv_other = late[:3]
    squares = project_state(gathered.ref(), state.ref(), weight, blocks, state_out.ref)
    state_out.send()
    inverse = normalize_rows(squares, state_out.ref, gain.ref(), normed.ref)
    normed.send()
    rows = dot(normed.ref[...], w_query.ref()[...]).astype(BF16)
    query.ref[...] = rows
    query.send()
    logs = attention(place[0], rows, (kv_mine.ref(), kv_other.ref()), scores, attended)
    lane = lax.broadcasted_iota(jnp.int32, logs.shape, 1)
    stats.ref[...] = jnp.where(lane == INVERSE, inverse, logs)
    stats.send()


def turn_kernel(loss_weight, place, early, late, raw, results, scratch):
    gathered, state = early
    weight, state_new, teacher, sems = scratch
    grad, grad_round, grad_attended, grad_query = results
    rows = state_new.shape[0]
    blocks = fetch_out_weight(place, raw[1:], weight, sems)
    below = pltpu.make_async_copy(raw[0].at[:, pl.ds(rows, rows), :], teacher, sems.at[sems.shape[0] - 1])
    below.start()
    start_all(late)
    kv_mine, kv_other, query, attended, logs, rider = late
    got = gathered.ref()
    project_state(got, state.ref(), weight, blocks, state_new)
    below.wait()
    width = got.shape[2]
    for i in range(got.shape[0]):
        columns = slice(i * width, (i + 1) * width)
        new = loss_weight * (state_new[:, columns] - teacher[i].astype(F32))
        grad.ref[:, columns] = new
        grad_round.ref[:, columns] = new.astype(BF16)
    grad.send()
    grad_round.send()
    send_below(grad_query, rider.ref())
    out = dot_nt(grad_round.ref[...], weight[place[1]]).astype(BF16)
    grad_attended.ref[...] = out
    grad_attended.send()
    attention_back(
        place[0], query.ref()[...], (kv_mine.ref(), kv_other.ref()), out, attended.ref()[...], logs.ref()[...], grad_query
    )


def norm_back(gathered, state, inv, gain, grad, loss_weight, weight, blocks, scratch, grad_out, round_out, gain_out):
    rows, model = state.shape
    count = gathered.shape[0]
    mean = jnp.zeros((rows, 1), F32)
    for copy, columns in blocks:
        copy.wait()
        normed = dot_nt(gathered[0, :rows, :], weight[0, columns, :])
        for h in range(1, count):
            normed = normed + dot_nt(gathered[h, :rows, :], weight[h, columns, :])
        term = normed * (state[:, columns] * inv)
        gain_out[:, columns] = jnp.broadcast_to(jnp.sum(term, axis=0, keepdims=True), (8, BLOCK))
        mean = mean + jnp.sum(term * gain[0:1, columns], axis=1, keepdims=True)
        scratch[:, columns] = normed
    mean = mean / model
    width = gathered.shape[2]
    for i in range(count):
        columns = slice(i * width, (i + 1) * width)
        here = state[:, columns]
        new = grad[:, columns] + inv * (scratch[:, columns] * gain[0:1, columns] - here * inv * mean)
        new = new + loss_weight * (here - gathered[i, rows:, :].astype(F32))
        grad_out[:, columns] = new
        round_out[:, columns] = new.astype(BF16)


def back_kernel(level, loss_weight, place, early, late, raw, results, scratch):
    gathered, state, stats, gain, grad = early
    weight, back, sems = scratch
    blocks = fetch_query_weight(place, raw, weight, sems)
    start_all(late)
    w_out, kv_mine, kv_other, query, attended, extra = late[:6]
    grad_out, grad_round, grad_attended, gain_out = results[:4]
    inv = stats.ref()[:, INVERSE : INVERSE + 1]
    norm_back(
        gathered.ref(), state.ref(), inv, gain.ref(), grad.ref(), loss_weight, weight, blocks, back,
        grad_out.ref, grad_round.ref, gain_out.ref,
    )
    grad_out.send()
    grad_round.send()
    gain_out.send()
    out = dot_nt(grad_round.ref[...], w_out.ref()[...]).astype(BF16)
    grad_attended.ref[...] = out
    grad_attended.send()
    kv = (kv_mine.ref(), kv_other.ref())
    if level > 0:
        send_below(results[4], late[6].ref())
        attention_back(place[0], query.ref()[...], kv, out, attended.ref()[...], extra.ref()[...], results[4])
        return
    half = kv[0].shape[0]

    def store(chunk, column, term):
        end = results[4] if chunk * CHUNK < half else results[5]
        first = chunk * CHUNK % half
        end.ref[first : first + CHUNK, :, column : column + DH] = term.astype(BF16)
        if chunk * CHUNK == half and column == 0:
            results[4].send()

    key_back(place[0], query.ref()[...], kv, out, attended.ref()[...], extra.ref()[...], late[6].ref(), store)
    results[5].send()


def keys_kernel(place, early, late, raw, results, scratch):
    query, grad_attended, attended, logs = [item.ref()[...] for item in early]
    start_all(late)
    kv = (late[0].ref(), late[1].ref())
    prior = late[2].ref() if len(late) > 2 else None
    sums = results[0]

    def store(chunk, column, term):
        sums.ref[chunk * CHUNK : (chunk + 1) * CHUNK, :, column : column + DH] = term

    key_back(place[0], query, kv, grad_attended, attended, logs, prior, store)
    sums.send()


def query_kernel(place, early, late, raw, results, scratch):
    query, grad_attended, attended, logs = [item.ref()[...] for item in early]
    start_all(late)
    kv_mine, kv_other = late[0].ref(), late[1].ref()
    grad_query, here, there = results
    attention_back(place[0], query, (kv_mine, kv_other), grad_attended, attended, logs, grad_query)
    refs = [item.ref() for item in late[2:]]
    count = (len(refs) - 2) // 4 + 1
    normeds, rounds, attendeds, queries = (
        refs[:count],
        refs[count : 2 * count],
        [attended] + refs[2 * count : 3 * count - 1],
        [grad_query.ref[...]] + refs[3 * count - 1 :],
    )
    width = query.shape[1]
    core = lax.rem(place[0], 2)
    slab = here.ref.shape[1]
    for end, parity in ((there, 1 - core), (here, core)):
        for i in range(end.ref.shape[0]):
            block = pl.ds(pl.multiple_of((2 * i + parity) * slab, slab), slab)
            for lhs, rhs, start in ((normeds, queries, 0), (rounds, attendeds, width)):
                total = dot_tn(lhs[0][:, block], rhs[0][...])
                for a, b in zip(lhs[1:], rhs[1:]):
                    total = total + dot_tn(a[:, block], b[...])
                end.ref[i, :, start : start + width] = total.astype(BF16)
        end.send()


def leave_kernel(place, early, late, raw, results, scratch):
    parts, grad_query, state, stats, gain, w_query, w_key, w_value, normed, *gain_terms = early
    there, here = results[:2]
    steps = results[2:]
    back = scratch[0]
    rows, model = back.shape
    width = grad_query.dst.shape[1]
    got = parts.ref()
    own = got[0].astype(F32)
    for i in range(1, got.shape[0]):
        own = own + got[i].astype(F32)
    own = own.astype(BF16)
    inv = stats.ref()[:, INVERSE : INVERSE + 1]
    head = place[1]
    mean = jnp.zeros((rows, 1), F32)
    gain_rows = []
    for start in range(0, model, BLOCK):
        columns = slice(start, start + BLOCK)
        part = dot_nt(grad_query.ref()[...], w_query.ref()[columns, :])
        part = part + dot_nt(own[:, :width], w_key.ref()[columns, :])
        part = part + dot_nt(own[:, width:], w_value.ref()[columns, :])
        term = part * (state.ref()[:, columns] * inv)
        feature = start + lax.broadcasted_iota(jnp.int32, (1, BLOCK), 1)
        mine = jnp.logical_and(feature >= head * width, feature < (head + 1) * width)
        before = gain_terms[0].ref()[0:1, columns]
        for term_before in gain_terms[1:]:
            before = before + term_before.ref()[0:1, columns]
        before = jnp.where(mine, before, 0.0)
        gain_rows.append(jnp.sum(term, axis=0, keepdims=True) + before)
        mean = mean + jnp.sum(term * gain.ref()[0:1, columns], axis=1, keepdims=True)
        back[:, columns] = part
    mean = mean / model
    count = here.ref.shape[0]
    slab = model // (2 * count)
    pad = here.ref.shape[1] - slab
    row = lax.broadcasted_iota(jnp.int32, (pad, BLOCK), 0)
    tail = jnp.zeros((pad, BLOCK), F32)
    for i, value in enumerate(gain_rows):
        tail = jnp.where(row == i, jnp.broadcast_to(value, tail.shape), tail)
    tail = tail.astype(BF16)
    core = lax.rem(place[0], 2)
    for end, parity in ((there, 1 - core), (here, core)):
        for i in range(count):
            block = pl.ds(pl.multiple_of((2 * i + parity) * slab, slab), slab)
            end.ref[i, :slab, :] = dot_tn(normed.ref()[:, block], own).astype(BF16)
            end.ref[i, slab:, :] = tail
        end.send()
    for k, step in enumerate(steps):
        columns = pl.ds(pl.multiple_of(lax.bitwise_xor(head, k) * width, width), width)
        factor = gain.ref()[0:1, columns]
        new = inv * (back[:, columns] * factor - state.ref()[:, columns] * inv * mean)
        step.ref[...] = new.astype(BF16)
        step.send()


def pair_kernel(place, early, late, raw, results, scratch):
    refs = [item.ref() for item in early]
    out = results[0]
    for i in range(out.ref.shape[0]):
        start = 0
        for here, there in zip(refs[::2], refs[1::2]):
            total = here[i].astype(F32) + there[i].astype(F32)
            out.ref[i, start : start + total.shape[0], :] = total.astype(BF16)
            start += total.shape[0]
    out.send()


def middle_kernel(place, early, late, raw, results, scratch):
    grad, sem = scratch
    rows, width = grad.shape
    columns = pl.ds(pl.multiple_of(place[1] * width, width), width)
    copy = pltpu.make_async_copy(raw[0].at[:, columns], grad, sem.at[0])
    copy.start()
    got = early[0].ref()
    gain, grad_input, grad_query, grad_out, grad_key, grad_value = results
    slab = grad_query.ref.shape[0]
    total = got[0].astype(F32)
    for i in range(1, got.shape[0]):
        total = total + got[i].astype(F32)
    row = lax.broadcasted_iota(jnp.int32, gain.ref.shape, 0)
    tail = jnp.zeros(gain.ref.shape, F32)
    for i in range(gain.out.shape[0]):
        value = total[2 * slab + i // 2 : 2 * slab + i // 2 + 1, (i % 2) * width : (i % 2 + 1) * width]
        tail = jnp.where(row == i, jnp.broadcast_to(value, tail.shape), tail)
    gain.ref[...] = tail.astype(BF16)
    gain.send(*[(gain.ref, gain.out.at[i]) for i in range(gain.out.shape[0])])
    grad_query.ref[...] = total[:slab, :width]
    grad_out.ref[...] = jnp.transpose(total[:slab, width:])
    grad_key.ref[...] = total[slab : 2 * slab, :width]
    grad_value.ref[...] = total[slab : 2 * slab, width:]
    for end in results[2:]:
        end.send()
    step = early[1].ref()[...].astype(F32)
    for item in early[2:]:
        step = step + item.ref()[...].astype(F32)
    copy.wait()
    grad_input.ref[...] = grad[...] + step
    grad_input.send()


def last_kernel(place, early, late, raw, results, scratch):
    got = early[0].ref()
    total = got[0].astype(F32)
    for i in range(1, got.shape[0]):
        total = total + got[i].astype(F32)
    results[0].ref[...] = total[: results[0].ref.shape[0]]
    results[0].send()


def body(tokens, norm_gain, w_query, w_key, w_value, w_out, teacher):
    rows, width = tokens.shape
    shards = lax.axis_size("ctx")
    heads = lax.axis_size("head")
    model = w_query.shape[0]
    chips = shards // 2
    slab = model // shards
    ctx = lax.axis_index("ctx")
    head = lax.axis_index("head")
    core = ctx % 2
    same_core = [[2 * i + c for i in range(chips)] for c in range(2)]
    sibling = [(i, i ^ 1) for i in range(shards)]
    loss_weight = 1.0 / math.sqrt(rows * shards)
    dma = pltpu.SemaphoreType.DMA

    def spread(x, count):
        return jnp.broadcast_to(x[None], (count,) + x.shape)

    def over_heads(x):
        return lax.all_to_all(x, "head", 0, 0)

    def over_chips(x):
        return lax.all_to_all(x, "ctx", 0, 0, axis_index_groups=same_core)

    def swap(x):
        return lax.ppermute(x, "ctx", sibling)

    def after(x, *others):
        return lax.optimization_barrier((x,) + others)[0]

    place = jnp.stack([ctx, head]).astype(jnp.int32)
    gain = jnp.broadcast_to(norm_gain.reshape(1, model), (8, model))

    out_mine = lax.all_gather(lax.dynamic_slice_in_dim(w_out, core * (width // 2), width // 2, 0), "head", axis=0)
    back_mine = lax.all_gather(lax.dynamic_slice_in_dim(w_query, core * (model // 2), model // 2, 0), "head", axis=0)
    first = over_heads(spread(tokens, heads))

    wide = same((rows, model), F32)
    thin = same((rows, model), BF16)
    own_shape = same((rows, width), BF16)
    sent = (shape((rows, width), BF16), shape((heads, rows, width), BF16), heads * (width // DH))
    taller = (shape((rows, width), BF16), shape((heads, 2 * rows, width), BF16), heads * (width // DH + 1))
    stats_shape = same((rows, DH), F32)
    score_scratch = pltpu.VMEM((rows, rows * shards), F32)
    weight_scratch = pltpu.VMEM((heads, width, model), BF16)
    back_scratch = pltpu.VMEM((heads, model, width), BF16)
    out_sems = 2 * (model // BLOCK)
    wide_scratch = pltpu.VMEM((rows, model), F32)
    pairs = rows * rows * shards * (width // DH)
    matmul = 2 * pairs * DH
    projection = 2 * rows * model * model
    small = projection // heads

    state, normed, stats, query, own = call(
        enter_kernel,
        [
            wide,
            thin,
            stats_shape,
            own_shape,
            (shape((rows, 2 * width), BF16), shape((chips, rows, 2 * width), BF16), 2 * chips),
        ],
        (3 * small, 8 << 20, 0),
        place, [first, gain, w_key, w_value, w_query],
    )
    kv_mine = over_chips(own)
    kv = [kv_mine, swap(kv_mine)]
    sent_rows, logs = call(
        first_kernel,
        [taller, stats_shape],
        (2 * matmul, 5 << 20, pairs),
        place, [query], [*kv, (teacher, RECUR - 1, rows)], scratch=[score_scratch],
    )
    states, normeds, queries, attendeds = [state], [normed], [query], [sent_rows]
    stats_list, logs_list = [stats], [logs]
    gathered_first = over_heads(sent_rows)
    out_mine = after(out_mine, gathered_first)
    out_raw = [out_mine, swap(out_mine)]
    for level in range(1, RECUR):
        state, normed, query, sent_rows, stats = call(
            level_kernel,
            [wide, thin, own_shape, sent, stats_shape],
            (projection + small + 2 * matmul, 18 << 20, pairs),
            place, [gathered_first if level == 1 else over_heads(sent_rows), states[-1], gain],
            [w_query, *kv], out_raw,
            [weight_scratch, score_scratch, dma((out_sems,))],
        )
        states.append(state)
        normeds.append(normed)
        queries.append(query)
        attendeds.append(sent_rows)
        stats_list.append(stats)
        logs_list.append(stats)
    own_attended = [(rows_, 0, rows) for rows_ in attendeds]

    gathered = over_heads(sent_rows)
    level = RECUR - 1
    grad, grad_round, grad_attended, sent_rows = call(
        functools.partial(turn_kernel, loss_weight),
        [wide, thin, own_shape, taller],
        (projection + small + 3 * matmul, 18 << 20, pairs),
        place, [gathered, states[level]],
        [*kv, queries[level], own_attended[level], logs_list[level], (teacher, level - 1, rows)],
        [gathered_first, *out_raw],
        [weight_scratch, wide_scratch, pltpu.VMEM((heads, rows, width), BF16), dma((out_sems + 1,))],
    )
    back_mine = after(back_mine, sent_rows)
    back_raw = [back_mine, swap(back_mine)]
    grad_rounds, grad_queries, grad_attendeds = [grad_round], [(sent_rows, 0, rows)], [grad_attended]
    gain_terms = []
    sums = []
    for level in range(RECUR - 2, -1, -1):
        gathered = over_heads(after(sent_rows, *sums) if sums else sent_rows)
        up = level + 1
        sums = call(
            keys_kernel,
            [same((shards, rows, 2 * width), F32)],
            (4 * matmul, 16 << 20, pairs),
            place, [queries[up], grad_attendeds[-1], own_attended[up], logs_list[up]], [*kv, *sums],
        )
        results = [wide, thin, own_shape, same((8, model), F32)]
        late = [w_out, *kv, queries[level], own_attended[level], logs_list[level]]
        if level > 0:
            results = results + [taller]
            late = late + [(teacher, level - 1, rows)]
        else:
            results = results + [same((chips, rows, 2 * width), BF16)] * 2
            late = late + list(sums)
        grad, grad_round, grad_attended, gain_term, sent_rows, *sent_other = call(
            functools.partial(back_kernel, level, loss_weight),
            results,
            (projection + small + 4 * matmul, 20 << 20, pairs),
            place, [gathered, states[up], stats_list[up], gain, grad], late, back_raw,
            [back_scratch, wide_scratch, dma((model // BLOCK,))],
        )
        gain_terms.append(gain_term)
        grad_rounds.append(grad_round)
        grad_attendeds.append(grad_attended)
        if level > 0:
            grad_queries.append((sent_rows, 0, rows))

    def add_pairs(*arrays):
        tall = sum(x.shape[1] for x in arrays[::2])
        total = same((chips, tall, 2 * width), BF16)
        return call(pair_kernel, [total], (1 << 20, 6 << 20, 0), place, arrays)[0]

    pair = (sent_rows.astype(F32) + swap(sent_other[0]).astype(F32)).astype(BF16)
    parts = over_chips(pair)
    query_first = after(queries[0], pair)
    last_query, here, there = call(
        query_kernel,
        [(own_shape[0], own_shape[1], width // DH)] + [same((chips, slab, 2 * width), BF16)] * 2,
        (5 * matmul, 16 << 20, pairs),
        place, [query_first, grad_attendeds[-1], own_attended[0], logs_list[0]],
        [*kv, *normeds, *grad_rounds[::-1], *own_attended[1:], *grad_queries[::-1]],
    )
    early = (here, swap(there))

    pad = 16
    there, here, *steps = call(
        leave_kernel,
        [same((chips, slab + pad, 2 * width), BF16)] * 2 + [own_shape] * heads,
        (6 * small, 12 << 20, 0),
        place,
        [parts, last_query, states[0], stats_list[0], gain, w_query, w_key, w_value, normeds[0], *gain_terms],
        scratch=[wide_scratch],
    )
    both = add_pairs(*early, here, swap(there))
    steps = [
        lax.ppermute(step, "head", [(i, i ^ k) for i in range(heads)]) if k else step for k, step in enumerate(steps)
    ]
    gain_rows, grad_input, grad_query, grad_out, grad_key, grad_value = call(
        middle_kernel,
        [
            (shape((pad, width), BF16), shape((heads, pad, width), BF16), heads),
            same((rows, width), F32),
            same((slab, width), F32),
            same((width, slab), F32),
            same((slab, width), F32),
            same((slab, width), F32),
        ],
        (1 << 20, 6 << 20, 0),
        place, [over_chips(both), *steps], raw=[grad], scratch=[pltpu.VMEM((rows, width), F32), dma((1,))],
    )
    grad_gain = call(
        last_kernel,
        [same((model // width, width), F32)],
        (1 << 16, 1 << 17, 0),
        place, [over_heads(gain_rows)],
    )[0]
    return (grad_input, grad_gain.reshape(-1), grad_query, grad_key, grad_value, grad_out)


def solution(mesh):
    return jax.shard_map(
        body,
        mesh=mesh,
        in_specs=(
            P("ctx", "head"),
            P(),
            P(None, "head"),
            P(None, "head"),
            P(None, "head"),
            P("head", None),
            P(None, "ctx", "head"),
        ),
        out_specs=(
            P("ctx", "head"),
            P(),
            P("ctx", "head"),
            P("ctx", "head"),
            P("ctx", "head"),
            P("head", "ctx"),
        ),
        check_vma=False,
    )
```

```python
import functools
import math

import jax
import jax.numpy as jnp
from jax import lax
from jax.experimental import pallas as pl
from jax.experimental.pallas import tpu as pltpu
from jax.sharding import PartitionSpec as P

DH = 128
RECUR = 3

EPSILON = 1e-06
MASKED = -1e30
F32 = jnp.float32
BF16 = jnp.bfloat16
SCALING = 1.0 / math.sqrt(DH)
LOG2E = math.log2(math.e)
SMEM = pl.BlockSpec(memory_space=pltpu.SMEM)
ANY = pl.BlockSpec(memory_space=pl.ANY)
BLOCK = 512
CHUNK = 4
INVERSE = 2


def dot(a, b):
    return jnp.dot(a, b, preferred_element_type=F32)


def dot_tn(a, b):
    return lax.dot_general(a, b, (((0,), (0,)), ((), ())), preferred_element_type=F32)


def dot_nt(a, b):
    return lax.dot_general(a, b, (((1,), (1,)), ((), ())), preferred_element_type=F32)


def shape(dims, kind):
    return jax.ShapeDtypeStruct(dims, kind)


class Fetched:
    def __init__(self, src, dst, sem):
        self.copy = pltpu.make_async_copy(src, dst, sem)
        self.dst = dst
        self.waited = False

    def start(self):
        self.copy.start()

    def ref(self):
        if not self.waited:
            self.copy.wait()
            self.waited = True
        return self.dst


class Result:
    def __init__(self, ref, out, sems):
        self.ref, self.out, self.sems, self.copies = ref, out, sems, []

    def send(self, *views):
        for src, dst in views or ((self.ref, self.out),):
            copy = pltpu.make_async_copy(src, dst, self.sems.at[len(self.copies)])
            copy.start()
            self.copies.append(copy)


def call(kernel, results, cost, place, early, late=(), raw=(), scratch=()):
    n_early, n_late, n_raw, n_out, n_scratch = len(early), len(late), len(raw), len(results), len(scratch)
    parts = [x[1:] if isinstance(x, tuple) else None for x in [*early, *late]]
    early, late = ([x[0] if isinstance(x, tuple) else x for x in group] for group in (early, late))

    def inner(*refs):
        refs = list(refs)

        def take(count):
            taken, refs[:] = refs[:count], refs[count:]
            return taken

        place_ref = take(1)[0]
        early_src, late_src, raw_ref, out = take(n_early), take(n_late), take(n_raw), take(n_out)
        early_src = [ref.at[part[0], 0 : part[1]] if part else ref for ref, part in zip(early_src, parts)]
        late_src = [ref.at[part[0], 0 : part[1]] if part else ref for ref, part in zip(late_src, parts[n_early:])]
        early_dst, late_dst, out_ref, more = take(n_early), take(n_late), take(n_out), take(n_scratch)
        in_sems, out_sems = refs[0], refs[1:]
        first = [Fetched(s, d, in_sems.at[i]) for i, (s, d) in enumerate(zip(early_src, early_dst))]
        then = [Fetched(s, d, in_sems.at[n_early + i]) for i, (s, d) in enumerate(zip(late_src, late_dst))]
        ends = [Result(r, o, s) for r, o, s in zip(out_ref, out, out_sems)]
        for item in first:
            item.start()
        kernel(place_ref, first, then, raw_ref, ends, more)
        for item in first + then:
            item.ref()
        for end in ends:
            for copy in end.copies:
                copy.wait()

    def vmem(x, part=None):
        return pltpu.VMEM((part[1], *x.shape[2:]) if part else x.shape, x.dtype)

    return pl.pallas_call(
        inner,
        out_shape=[r[1] for r in results],
        in_specs=[SMEM] + [ANY] * (n_early + n_late + n_raw),
        out_specs=[pl.BlockSpec(memory_space=pltpu.HBM)] * n_out,
        scratch_shapes=[vmem(x, part) for x, part in zip([*early, *late], parts)]
        + [vmem(r[0]) for r in results]
        + list(scratch)
        + [pltpu.SemaphoreType.DMA((max(1, n_early + n_late),))]
        + [pltpu.SemaphoreType.DMA((r[2],)) for r in results],
        compiler_params=pltpu.CompilerParams(vmem_limit_bytes=52 * 1024 * 1024),
        cost_estimate=pl.CostEstimate(flops=cost[0], bytes_accessed=cost[1], transcendentals=cost[2]),
    )(place, *early, *late, *raw)


def same(dims, kind):
    return (shape(dims, kind), shape(dims, kind), 1)


def start_all(items):
    for item in items:
        item.start()


def fetch_out_weight(place, raw, weight, sems):
    core = lax.rem(place[0], 2)
    half = raw[0].shape[1]
    blocks = []
    for start in range(0, raw[0].shape[2], BLOCK):
        columns = pl.ds(start, BLOCK)
        block = []
        group = 0
        for j, ref in enumerate(raw):
            parity = core if j == 0 else 1 - core
            rows = pl.ds(pl.multiple_of(parity * half, half), half)
            sem = sems.at[len(raw) * (start // BLOCK) + j]
            groups = pl.ds(group, ref.shape[0])
            block.append(pltpu.make_async_copy(ref.at[:, :, columns], weight.at[groups, rows, columns], sem))
            group = group + ref.shape[0] if j else 0
        start_all(block)
        blocks.append(block)
    return blocks


def fetch_query_weight(place, raw, weight, sems):
    core = lax.rem(place[0], 2)
    half = raw[0].shape[1]
    blocks = []
    for ref, parity in ((raw[0], core), (raw[1], 1 - core)):
        for start in range(0, half, BLOCK):
            rows = pl.ds(pl.multiple_of(parity * half + start, BLOCK), BLOCK)
            copy = pltpu.make_async_copy(ref.at[:, pl.ds(start, BLOCK), :], weight.at[:, rows, :], sems.at[len(blocks)])
            copy.start()
            blocks.append((copy, rows))
    return blocks


def wait_all(copies):
    for copy in copies:
        copy.wait()


def lanes_joined(ref, rows):
    return jnp.concatenate([ref[i, :rows, :] for i in range(ref.shape[0])], axis=1)


def key_position(shape_, axis, rows, chunk, half, core):
    index = lax.broadcasted_iota(jnp.int32, shape_, axis)
    gap = jnp.zeros(shape_, jnp.int32)
    for i in range(1, CHUNK):
        gap = gap + jnp.where(index >= i * rows, rows, 0)
    first = chunk * CHUNK
    start = 2 * (first % half) * rows + (core if first < half else 1 - core) * rows
    return index + gap + start


def chunk_of(kv, chunk, column):
    half = kv[0].shape[0]
    ref = kv[0] if chunk * CHUNK < half else kv[1]
    first = chunk * CHUNK % half
    return ref[first : first + CHUNK, :, column : column + DH].reshape(-1, DH)


def chunks_of(kv):
    return 2 * kv[0].shape[0] // CHUNK


def send_spread(result, cut):
    if len(result.out.shape) == 2:
        result.send((result.ref.at[:, cut], result.out.at[:, cut]))
        return
    rows = slice(0, result.ref.shape[0])
    result.send(*[(result.ref.at[:, cut], result.out.at[i, rows, cut]) for i in range(result.out.shape[0])])


def send_below(result, rider):
    rows = pl.ds(result.ref.shape[0], rider.shape[0])
    result.send(*[(rider, result.out.at[i, rows, :]) for i in range(result.out.shape[0])])


def attention(ctx, query, kv, scores, attended):
    rows, width = query.shape
    core = lax.rem(ctx, 2)
    span = CHUNK * rows
    query_pos = ctx * rows + lax.broadcasted_iota(jnp.int32, (rows, 1), 0)
    lane = lax.broadcasted_iota(jnp.int32, (rows, DH), 1)
    logs = jnp.zeros((rows, DH), F32)
    for head in range(width // DH):
        cut = slice(head * DH, (head + 1) * DH)
        rows_q = query[:, cut]
        row_max = jnp.full((rows, 1), MASKED, F32)
        for chunk in range(chunks_of(kv)):
            key_pos = key_position((1, span), 1, rows, chunk, kv[0].shape[0], core)
            part = dot_nt(rows_q, chunk_of(kv, chunk, head * DH)) * (SCALING * LOG2E)
            part = jnp.where(key_pos <= query_pos, part, MASKED)
            scores[:, chunk * span : (chunk + 1) * span] = part
            row_max = jnp.maximum(row_max, jnp.max(part, axis=1, keepdims=True))
        total = jnp.zeros((rows, 1), F32)
        out = jnp.zeros((rows, DH), F32)
        for chunk in range(chunks_of(kv)):
            part = jnp.exp2(scores[:, chunk * span : (chunk + 1) * span] - row_max)
            total = total + jnp.sum(part, axis=1, keepdims=True)
            out = out + dot(part.astype(BF16), chunk_of(kv, chunk, width + head * DH))
        attended.ref[:, cut] = (out / total).astype(BF16)
        send_spread(attended, cut)
        logs = jnp.where(lane == head, row_max + jnp.log2(total), logs)
    return logs


def attention_back(ctx, query, kv, grad_attended, attended, logs, grad_query):
    rows, width = query.shape
    core = lax.rem(ctx, 2)
    span = CHUNK * rows
    query_pos = ctx * rows + lax.broadcasted_iota(jnp.int32, (rows, 1), 0)
    for head in range(width // DH):
        cut = slice(head * DH, (head + 1) * DH)
        rows_q, rows_g = query[:, cut], grad_attended[:, cut]
        row_dot = jnp.sum(rows_g.astype(F32) * attended[:, cut].astype(F32), axis=1, keepdims=True)
        log_total = logs[:, head : head + 1]
        out = jnp.zeros((rows, DH), F32)
        for chunk in range(chunks_of(kv)):
            key_pos = key_position((1, span), 1, rows, chunk, kv[0].shape[0], core)
            keys = chunk_of(kv, chunk, head * DH)
            part = dot_nt(rows_q, keys) * (SCALING * LOG2E)
            part = jnp.exp2(jnp.where(key_pos <= query_pos, part, MASKED) - log_total)
            grad_probs = dot_nt(rows_g, chunk_of(kv, chunk, width + head * DH))
            out = out + dot((part * (grad_probs - row_dot)).astype(BF16), keys)
        grad_query.ref[:, cut] = (out * SCALING).astype(BF16)
        send_spread(grad_query, cut)


def turned(picks, columns):
    total = jnp.zeros((picks.shape[0], columns.shape[0]), F32)
    for _ in range(3):
        piece = columns.astype(BF16)
        columns = columns - piece.astype(F32)
        total = total + dot_nt(picks, piece)
    return total


def key_back(ctx, query, kv, grad_attended, attended, logs, prior, store):
    rows, width = query.shape
    core = lax.rem(ctx, 2)
    span = CHUNK * rows
    query_pos = ctx * rows + lax.broadcasted_iota(jnp.int32, (1, rows), 1)
    picks = (lax.broadcasted_iota(jnp.int32, (8, DH), 0) == lax.broadcasted_iota(jnp.int32, (8, DH), 1)).astype(BF16)
    log_rows = turned(picks, logs)
    row_dots = []
    for head in range(width // DH):
        cut = slice(head * DH, (head + 1) * DH)
        product = grad_attended[:, cut].astype(F32) * attended[:, cut].astype(F32)
        row_dots.append(turned(jnp.ones((8, DH), BF16), product)[0:1])
    for chunk in range(chunks_of(kv)):
        key_pos = key_position((span, 1), 0, rows, chunk, kv[0].shape[0], core)
        for head in range(width // DH):
            cut = slice(head * DH, (head + 1) * DH)
            rows_q, rows_g = query[:, cut], grad_attended[:, cut]
            part = dot_nt(chunk_of(kv, chunk, head * DH), rows_q) * (SCALING * LOG2E)
            part = jnp.exp2(jnp.where(key_pos <= query_pos, part, MASKED) - log_rows[head : head + 1, :])
            grad_probs = dot_nt(chunk_of(kv, chunk, width + head * DH), rows_g)
            key_term = dot((part * (grad_probs - row_dots[head])).astype(BF16), rows_q) * SCALING
            value_term = dot(part.astype(BF16), rows_g)
            for term, column in ((key_term, head * DH), (value_term, width + head * DH)):
                term = term.reshape(CHUNK, rows, DH)
                if prior is not None:
                    term = term + prior[chunk * CHUNK : (chunk + 1) * CHUNK, :, column : column + DH]
                store(chunk, column, term)


def project_state(gathered, state, weight, blocks, state_out):
    whole = lanes_joined(gathered, state.shape[0])
    squares = jnp.zeros((whole.shape[0], 1), F32)
    for start in range(0, state.shape[1], BLOCK):
        wait_all(blocks[start // BLOCK])
        columns = slice(start, start + BLOCK)
        new = state[:, columns] + dot(whole, weight[:, :, columns].reshape(whole.shape[1], BLOCK))
        state_out[:, columns] = new
        squares = squares + jnp.sum(new * new, axis=1, keepdims=True)
    return squares


def normalize_rows(squares, state, gain, normed):
    model = state.shape[1]
    inverse = lax.rsqrt(squares / model + EPSILON)
    for start in range(0, model, BLOCK):
        columns = slice(start, start + BLOCK)
        normed[:, columns] = (state[:, columns] * inverse * gain[0:1, columns]).astype(BF16)
    return inverse


def enter_kernel(place, early, late, raw, results, scratch):
    gathered, gain, w_key, w_value, w_query = early
    state, normed, stats, query, own = results
    rows = state.ref.shape[0]
    squares = jnp.zeros((rows, 1), F32)
    got = gathered.ref()
    width = got.shape[2]
    for i in range(got.shape[0]):
        part = got[i].astype(F32)
        state.ref[:, i * width : (i + 1) * width] = part
        squares = squares + jnp.sum(part * part, axis=1, keepdims=True)
    state.send()
    inverse = normalize_rows(squares, state.ref, gain.ref(), normed.ref)
    normed.send()
    stats.ref[...] = jnp.broadcast_to(inverse, stats.ref.shape)
    stats.send()
    for weight, cut in ((w_key, slice(0, width)), (w_value, slice(width, 2 * width))):
        own.ref[:, cut] = dot(normed.ref[...], weight.ref()[...]).astype(BF16)
        send_spread(own, cut)
    query.ref[...] = dot(normed.ref[...], w_query.ref()[...]).astype(BF16)
    query.send()


def first_kernel(place, early, late, raw, results, scratch):
    query = early[0].ref()[...]
    start_all(late)
    attended, stats = results
    send_below(attended, late[2].ref())
    stats.ref[...] = attention(place[0], query, (late[0].ref(), late[1].ref()), scratch[0], attended)
    stats.send()


def level_kernel(place, early, late, raw, results, scratch):
    gathered, state, gain = early
    weight, scores, sems = scratch
    state_out, normed, query, attended, stats = results
    blocks = fetch_out_weight(place, raw, weight, sems)
    start_all(late)
    w_query, kv_mine, kv_other = late[:3]
    squares = project_state(gathered.ref(), state.ref(), weight, blocks, state_out.ref)
    state_out.send()
    inverse = normalize_rows(squares, state_out.ref, gain.ref(), normed.ref)
    normed.send()
    rows = dot(normed.ref[...], w_query.ref()[...]).astype(BF16)
    query.ref[...] = rows
    query.send()
    logs = attention(place[0], rows, (kv_mine.ref(), kv_other.ref()), scores, attended)
    lane = lax.broadcasted_iota(jnp.int32, logs.shape, 1)
    stats.ref[...] = jnp.where(lane == INVERSE, inverse, logs)
    stats.send()


def turn_kernel(loss_weight, place, early, late, raw, results, scratch):
    gathered, state = early
    weight, state_new, teacher, sems = scratch
    grad, grad_round, grad_attended, grad_query = results
    rows = state_new.shape[0]
    blocks = fetch_out_weight(place, raw[1:], weight, sems)
    below = pltpu.make_async_copy(raw[0].at[:, pl.ds(rows, rows), :], teacher, sems.at[sems.shape[0] - 1])
    below.start()
    start_all(late)
    kv_mine, kv_other, query, attended, logs, rider = late
    got = gathered.ref()
    project_state(got, state.ref(), weight, blocks, state_new)
    below.wait()
    width = got.shape[2]
    for i in range(got.shape[0]):
        columns = slice(i * width, (i + 1) * width)
        new = loss_weight * (state_new[:, columns] - teacher[i].astype(F32))
        grad.ref[:, columns] = new
        grad_round.ref[:, columns] = new.astype(BF16)
    grad.send()
    grad_round.send()
    send_below(grad_query, rider.ref())
    out = dot_nt(grad_round.ref[...], weight[place[1]]).astype(BF16)
    grad_attended.ref[...] = out
    grad_attended.send()
    attention_back(
        place[0], query.ref()[...], (kv_mine.ref(), kv_other.ref()), out, attended.ref()[...], logs.ref()[...], grad_query
    )


def norm_back(gathered, state, inv, gain, grad, loss_weight, weight, blocks, scratch, grad_out, round_out, gain_out):
    rows, model = state.shape
    count = gathered.shape[0]
    mean = jnp.zeros((rows, 1), F32)
    for copy, columns in blocks:
        copy.wait()
        normed = dot_nt(gathered[0, :rows, :], weight[0, columns, :])
        for h in range(1, count):
            normed = normed + dot_nt(gathered[h, :rows, :], weight[h, columns, :])
        term = normed * (state[:, columns] * inv)
        gain_out[:, columns] = jnp.broadcast_to(jnp.sum(term, axis=0, keepdims=True), (8, BLOCK))
        mean = mean + jnp.sum(term * gain[0:1, columns], axis=1, keepdims=True)
        scratch[:, columns] = normed
    mean = mean / model
    width = gathered.shape[2]
    for i in range(count):
        columns = slice(i * width, (i + 1) * width)
        here = state[:, columns]
        new = grad[:, columns] + inv * (scratch[:, columns] * gain[0:1, columns] - here * inv * mean)
        new = new + loss_weight * (here - gathered[i, rows:, :].astype(F32))
        grad_out[:, columns] = new
        round_out[:, columns] = new.astype(BF16)


def back_kernel(level, loss_weight, place, early, late, raw, results, scratch):
    gathered, state, stats, gain, grad = early
    weight, back, sems = scratch
    blocks = fetch_query_weight(place, raw, weight, sems)
    start_all(late)
    w_out, kv_mine, kv_other, query, attended, extra = late[:6]
    grad_out, grad_round, grad_attended, gain_out = results[:4]
    inv = stats.ref()[:, INVERSE : INVERSE + 1]
    norm_back(
        gathered.ref(), state.ref(), inv, gain.ref(), grad.ref(), loss_weight, weight, blocks, back,
        grad_out.ref, grad_round.ref, gain_out.ref,
    )
    grad_out.send()
    grad_round.send()
    gain_out.send()
    out = dot_nt(grad_round.ref[...], w_out.ref()[...]).astype(BF16)
    grad_attended.ref[...] = out
    grad_attended.send()
    kv = (kv_mine.ref(), kv_other.ref())
    if level > 0:
        send_below(results[4], late[6].ref())
        attention_back(place[0], query.ref()[...], kv, out, attended.ref()[...], extra.ref()[...], results[4])
        return
    half = kv[0].shape[0]

    def store(chunk, column, term):
        end = results[4] if chunk * CHUNK < half else results[5]
        first = chunk * CHUNK % half
        end.ref[first : first + CHUNK, :, column : column + DH] = term.astype(BF16)
        if chunk * CHUNK == half and column == 0:
            results[4].send()

    key_back(place[0], query.ref()[...], kv, out, attended.ref()[...], extra.ref()[...], late[6].ref(), store)
    results[5].send()


def keys_kernel(place, early, late, raw, results, scratch):
    query, grad_attended, attended, logs = [item.ref()[...] for item in early]
    start_all(late)
    kv = (late[0].ref(), late[1].ref())
    prior = late[2].ref() if len(late) > 2 else None
    sums = results[0]

    def store(chunk, column, term):
        sums.ref[chunk * CHUNK : (chunk + 1) * CHUNK, :, column : column + DH] = term

    key_back(place[0], query, kv, grad_attended, attended, logs, prior, store)
    sums.send()


def query_kernel(place, early, late, raw, results, scratch):
    query, grad_attended, attended, logs = [item.ref()[...] for item in early]
    start_all(late)
    kv_mine, kv_other = late[0].ref(), late[1].ref()
    grad_query, here, there = results
    attention_back(place[0], query, (kv_mine, kv_other), grad_attended, attended, logs, grad_query)
    refs = [item.ref() for item in late[2:]]
    count = (len(refs) - 2) // 4 + 1
    normeds, rounds, attendeds, queries = (
        refs[:count],
        refs[count : 2 * count],
        [attended] + refs[2 * count : 3 * count - 1],
        [grad_query.ref[...]] + refs[3 * count - 1 :],
    )
    width = query.shape[1]
    core = lax.rem(place[0], 2)
    slab = here.ref.shape[1]
    for end, parity in ((there, 1 - core), (here, core)):
        for i in range(end.ref.shape[0]):
            block = pl.ds(pl.multiple_of((2 * i + parity) * slab, slab), slab)
            for lhs, rhs, start in ((normeds, queries, 0), (rounds, attendeds, width)):
                total = dot_tn(lhs[0][:, block], rhs[0][...])
                for a, b in zip(lhs[1:], rhs[1:]):
                    total = total + dot_tn(a[:, block], b[...])
                end.ref[i, :, start : start + width] = total.astype(BF16)
        end.send()


def leave_kernel(place, early, late, raw, results, scratch):
    parts, grad_query, state, stats, gain, w_query, w_key, w_value, normed, *gain_terms = early
    there, here = results[:2]
    steps = results[2:]
    back = scratch[0]
    rows, model = back.shape
    width = grad_query.dst.shape[1]
    got = parts.ref()
    own = got[0].astype(F32)
    for i in range(1, got.shape[0]):
        own = own + got[i].astype(F32)
    own = own.astype(BF16)
    inv = stats.ref()[:, INVERSE : INVERSE + 1]
    head = place[1]
    mean = jnp.zeros((rows, 1), F32)
    gain_rows = []
    for start in range(0, model, BLOCK):
        columns = slice(start, start + BLOCK)
        part = dot_nt(grad_query.ref()[...], w_query.ref()[columns, :])
        part = part + dot_nt(own[:, :width], w_key.ref()[columns, :])
        part = part + dot_nt(own[:, width:], w_value.ref()[columns, :])
        term = part * (state.ref()[:, columns] * inv)
        feature = start + lax.broadcasted_iota(jnp.int32, (1, BLOCK), 1)
        mine = jnp.logical_and(feature >= head * width, feature < (head + 1) * width)
        before = gain_terms[0].ref()[0:1, columns]
        for term_before in gain_terms[1:]:
            before = before + term_before.ref()[0:1, columns]
        before = jnp.where(mine, before, 0.0)
        gain_rows.append(jnp.sum(term, axis=0, keepdims=True) + before)
        mean = mean + jnp.sum(term * gain.ref()[0:1, columns], axis=1, keepdims=True)
        back[:, columns] = part
    mean = mean / model
    count = here.ref.shape[0]
    slab = model // (2 * count)
    pad = here.ref.shape[1] - slab
    row = lax.broadcasted_iota(jnp.int32, (pad, BLOCK), 0)
    tail = jnp.zeros((pad, BLOCK), F32)
    for i, value in enumerate(gain_rows):
        tail = jnp.where(row == i, jnp.broadcast_to(value, tail.shape), tail)
    tail = tail.astype(BF16)
    core = lax.rem(place[0], 2)
    for end, parity in ((there, 1 - core), (here, core)):
        for i in range(count):
            block = pl.ds(pl.multiple_of((2 * i + parity) * slab, slab), slab)
            end.ref[i, :slab, :] = dot_tn(normed.ref()[:, block], own).astype(BF16)
            end.ref[i, slab:, :] = tail
        end.send()
    for k, step in enumerate(steps):
        columns = pl.ds(pl.multiple_of(lax.bitwise_xor(head, k) * width, width), width)
        factor = gain.ref()[0:1, columns]
        new = inv * (back[:, columns] * factor - state.ref()[:, columns] * inv * mean)
        step.ref[...] = new.astype(BF16)
        step.send()


def pair_kernel(place, early, late, raw, results, scratch):
    refs = [item.ref() for item in early]
    out = results[0]
    for i in range(out.ref.shape[0]):
        start = 0
        for here, there in zip(refs[::2], refs[1::2]):
            total = here[i].astype(F32) + there[i].astype(F32)
            out.ref[i, start : start + total.shape[0], :] = total.astype(BF16)
            start += total.shape[0]
        out.send((out.ref.at[i], out.out.at[i]))


def middle_kernel(place, early, late, raw, results, scratch):
    grad, sem = scratch
    rows, width = grad.shape
    columns = pl.ds(pl.multiple_of(place[1] * width, width), width)
    copy = pltpu.make_async_copy(raw[0].at[:, columns], grad, sem.at[0])
    copy.start()
    got = early[0].ref()
    gain, grad_input, grad_query, grad_out, grad_key, grad_value = results
    slab = grad_query.ref.shape[0]
    total = got[0].astype(F32)
    for i in range(1, got.shape[0]):
        total = total + got[i].astype(F32)
    row = lax.broadcasted_iota(jnp.int32, gain.ref.shape, 0)
    tail = jnp.zeros(gain.ref.shape, F32)
    for i in range(gain.out.shape[0]):
        value = total[2 * slab + i // 2 : 2 * slab + i // 2 + 1, (i % 2) * width : (i % 2 + 1) * width]
        tail = jnp.where(row == i, jnp.broadcast_to(value, tail.shape), tail)
    gain.ref[...] = tail.astype(BF16)
    gain.send(*[(gain.ref, gain.out.at[i]) for i in range(gain.out.shape[0])])
    grad_query.ref[...] = total[:slab, :width]
    grad_out.ref[...] = jnp.transpose(total[:slab, width:])
    grad_key.ref[...] = total[slab : 2 * slab, :width]
    grad_value.ref[...] = total[slab : 2 * slab, width:]
    for end in results[2:]:
        end.send()
    step = early[1].ref()[...].astype(F32)
    for item in early[2:]:
        step = step + item.ref()[...].astype(F32)
    copy.wait()
    grad_input.ref[...] = grad[...] + step
    grad_input.send()


def last_kernel(place, early, late, raw, results, scratch):
    got = early[0].ref()
    total = got[0].astype(F32)
    for i in range(1, got.shape[0]):
        total = total + got[i].astype(F32)
    results[0].ref[...] = total[: results[0].ref.shape[0]]
    results[0].send()


def body(tokens, norm_gain, w_query, w_key, w_value, w_out, teacher):
    rows, width = tokens.shape
    shards = lax.axis_size("ctx")
    heads = lax.axis_size("head")
    model = w_query.shape[0]
    chips = shards // 2
    slab = model // shards
    ctx = lax.axis_index("ctx")
    head = lax.axis_index("head")
    core = ctx % 2
    same_core = [[2 * i + c for i in range(chips)] for c in range(2)]
    sibling = [(i, i ^ 1) for i in range(shards)]
    loss_weight = 1.0 / math.sqrt(rows * shards)
    dma = pltpu.SemaphoreType.DMA

    def spread(x, count):
        return jnp.broadcast_to(x[None], (count,) + x.shape)

    def over_heads(x):
        return lax.all_to_all(x, "head", 0, 0)

    def over_chips(x):
        return lax.all_to_all(x, "ctx", 0, 0, axis_index_groups=same_core)

    def swap(x):
        return lax.ppermute(x, "ctx", sibling)

    def after(x, *others):
        return lax.optimization_barrier((x,) + others)[0]

    place = jnp.stack([ctx, head]).astype(jnp.int32)
    gain = jnp.broadcast_to(norm_gain.reshape(1, model), (8, model))

    out_mine = lax.all_gather(lax.dynamic_slice_in_dim(w_out, core * (width // 2), width // 2, 0), "head", axis=0)
    back_mine = lax.all_gather(lax.dynamic_slice_in_dim(w_query, core * (model // 2), model // 2, 0), "head", axis=0)
    first = over_heads(spread(tokens, heads))

    wide = same((rows, model), F32)
    thin = same((rows, model), BF16)
    own_shape = same((rows, width), BF16)
    sent = (shape((rows, width), BF16), shape((heads, rows, width), BF16), heads * (width // DH))
    taller = (shape((rows, width), BF16), shape((heads, 2 * rows, width), BF16), heads * (width // DH + 1))
    stats_shape = same((rows, DH), F32)
    score_scratch = pltpu.VMEM((rows, rows * shards), F32)
    weight_scratch = pltpu.VMEM((heads, width, model), BF16)
    back_scratch = pltpu.VMEM((heads, model, width), BF16)
    out_sems = 2 * (model // BLOCK)
    wide_scratch = pltpu.VMEM((rows, model), F32)
    pairs = rows * rows * shards * (width // DH)
    matmul = 2 * pairs * DH
    projection = 2 * rows * model * model
    small = projection // heads

    state, normed, stats, query, own = call(
        enter_kernel,
        [
            wide,
            thin,
            stats_shape,
            own_shape,
            (shape((rows, 2 * width), BF16), shape((chips, rows, 2 * width), BF16), 2 * chips),
        ],
        (3 * small, 8 << 20, 0),
        place, [first, gain, w_key, w_value, w_query],
    )
    kv_mine = over_chips(own)
    kv = [kv_mine, swap(kv_mine)]
    sent_rows, logs = call(
        first_kernel,
        [taller, stats_shape],
        (2 * matmul, 5 << 20, pairs),
        place, [query], [*kv, (teacher, RECUR - 1, rows)], scratch=[score_scratch],
    )
    states, normeds, queries, attendeds = [state], [normed], [query], [sent_rows]
    stats_list, logs_list = [stats], [logs]
    gathered_first = over_heads(sent_rows)
    out_mine = after(out_mine, gathered_first)
    out_raw = [out_mine, swap(out_mine)]
    for level in range(1, RECUR):
        state, normed, query, sent_rows, stats = call(
            level_kernel,
            [wide, thin, own_shape, sent, stats_shape],
            (projection + small + 2 * matmul, 18 << 20, pairs),
            place, [gathered_first if level == 1 else over_heads(sent_rows), states[-1], gain],
            [w_query, *kv], out_raw,
            [weight_scratch, score_scratch, dma((out_sems,))],
        )
        states.append(state)
        normeds.append(normed)
        queries.append(query)
        attendeds.append(sent_rows)
        stats_list.append(stats)
        logs_list.append(stats)
    own_attended = [(rows_, 0, rows) for rows_ in attendeds]

    gathered = over_heads(sent_rows)
    level = RECUR - 1
    grad, grad_round, grad_attended, sent_rows = call(
        functools.partial(turn_kernel, loss_weight),
        [wide, thin, own_shape, taller],
        (projection + small + 3 * matmul, 18 << 20, pairs),
        place, [gathered, states[level]],
        [*kv, queries[level], own_attended[level], logs_list[level], (teacher, level - 1, rows)],
        [gathered_first, *out_raw],
        [weight_scratch, wide_scratch, pltpu.VMEM((heads, rows, width), BF16), dma((out_sems + 1,))],
    )
    back_mine = after(back_mine, sent_rows)
    back_raw = [back_mine, swap(back_mine)]
    grad_rounds, grad_queries, grad_attendeds = [grad_round], [(sent_rows, 0, rows)], [grad_attended]
    gain_terms = []
    sums = []
    for level in range(RECUR - 2, -1, -1):
        gathered = over_heads(after(sent_rows, *sums) if sums else sent_rows)
        up = level + 1
        sums = call(
            keys_kernel,
            [same((shards, rows, 2 * width), F32)],
            (4 * matmul, 16 << 20, pairs),
            place, [queries[up], grad_attendeds[-1], own_attended[up], logs_list[up]], [*kv, *sums],
        )
        results = [wide, thin, own_shape, same((8, model), F32)]
        late = [w_out, *kv, queries[level], own_attended[level], logs_list[level]]
        if level > 0:
            results = results + [taller]
            late = late + [(teacher, level - 1, rows)]
        else:
            results = results + [same((chips, rows, 2 * width), BF16)] * 2
            late = late + list(sums)
        grad, grad_round, grad_attended, gain_term, sent_rows, *sent_other = call(
            functools.partial(back_kernel, level, loss_weight),
            results,
            (projection + small + 4 * matmul, 20 << 20, pairs),
            place, [gathered, states[up], stats_list[up], gain, grad], late, back_raw,
            [back_scratch, wide_scratch, dma((model // BLOCK,))],
        )
        gain_terms.append(gain_term)
        grad_rounds.append(grad_round)
        grad_attendeds.append(grad_attended)
        if level > 0:
            grad_queries.append((sent_rows, 0, rows))

    def add_pairs(*arrays):
        tall = sum(x.shape[1] for x in arrays[::2])
        total = same((chips, tall, 2 * width), BF16)[:2] + (chips,)
        return call(pair_kernel, [total], (1 << 20, 6 << 20, 0), place, arrays)[0]

    pair = (sent_rows.astype(F32) + swap(sent_other[0]).astype(F32)).astype(BF16)
    parts = over_chips(pair)
    query_first = after(queries[0], pair)
    last_query, here, there = call(
        query_kernel,
        [(own_shape[0], own_shape[1], width // DH)] + [same((chips, slab, 2 * width), BF16)] * 2,
        (5 * matmul, 16 << 20, pairs),
        place, [query_first, grad_attendeds[-1], own_attended[0], logs_list[0]],
        [*kv, *normeds, *grad_rounds[::-1], *own_attended[1:], *grad_queries[::-1]],
    )
    early = (here, swap(there))

    pad = 16
    there, here, *steps = call(
        leave_kernel,
        [same((chips, slab + pad, 2 * width), BF16)] * 2 + [own_shape] * heads,
        (6 * small, 12 << 20, 0),
        place,
        [parts, last_query, states[0], stats_list[0], gain, w_query, w_key, w_value, normeds[0], *gain_terms],
        scratch=[wide_scratch],
    )
    both = add_pairs(*early, here, swap(there))
    steps = [
        lax.ppermute(step, "head", [(i, i ^ k) for i in range(heads)]) if k else step for k, step in enumerate(steps)
    ]
    gain_rows, grad_input, grad_query, grad_out, grad_key, grad_value = call(
        middle_kernel,
        [
            (shape((pad, width), BF16), shape((heads, pad, width), BF16), heads),
            same((rows, width), F32),
            same((slab, width), F32),
            same((width, slab), F32),
            same((slab, width), F32),
            same((slab, width), F32),
        ],
        (1 << 20, 6 << 20, 0),
        place, [over_chips(both), *steps], raw=[grad], scratch=[pltpu.VMEM((rows, width), F32), dma((1,))],
    )
    grad_gain = call(
        last_kernel,
        [same((model // width, width), F32)],
        (1 << 16, 1 << 17, 0),
        place, [over_heads(gain_rows)],
    )[0]
    return (grad_input, grad_gain.reshape(-1), grad_query, grad_key, grad_value, grad_out)


def solution(mesh):
    return jax.shard_map(
        body,
        mesh=mesh,
        in_specs=(
            P("ctx", "head"),
            P(),
            P(None, "head"),
            P(None, "head"),
            P(None, "head"),
            P("head", None),
            P(None, "ctx", "head"),
        ),
        out_specs=(
            P("ctx", "head"),
            P(),
            P("ctx", "head"),
            P("ctx", "head"),
            P("ctx", "head"),
            P("head", "ctx"),
        ),
        check_vma=False,
    )
```
